32 devices in a mesh: slab: 16 (over z, y, x), shot: 2 (over core).
Axes of the slice: x: 2, y: 2, z: 4, core: 2. Of those that a mesh axis runs over, the one named last changes fastest.
Arguments:
- pressure_init: float32 [4, 128, 32, 256], P('shot', 'slab'), may hold values from -6 to 6
- adjoint_init: float32 [4, 128, 32, 256], P('shot', 'slab'), may hold values from -1.5 to 1.5
- density: float32 [128, 32, 256], P('slab'), may hold values from 0.5 to 2
- speed: float32 [128, 32, 256], P('slab'), may hold values from 0.6 to 1.1
- admittance: float32 [128, 32, 256], P('slab'), may hold values from 0.05 to 0.5
- bound_mask: int32 [128, 32, 256], P('slab'), may hold values 0 or 1
- rec_cells: int32 [48, 32], P('slab'), may hold values from 0 to 65535, as said below
- rec_live: int32 [48], P('slab'), may hold values from 0 to 1, as said below
- encoder: float32 [32, 25], replicated, may hold values from -1 to 1
- target: float32 [48, 4, 2, 25], P('slab', 'shot'), may hold values from -6 to 6
Outputs:
- recording: float32 [48, 4, 2, 25], P('slab', 'shot')
- gradient: float32 [128, 32, 256], P('slab')
The draws below stay inside these ranges and needn't reach their ends.
Inputs may be any that keep to these rules, and one draw needn't show every extreme that they name: `rec_live`: in each aligned group of four slabs the numbers of live slots are 3, 1, 0 and 0 in an order drawn from the seed; a slab's live slots come first. `rec_cells`: each slot's 32 capsule cells form a block of 2 x 4 x 4 cells (z, x, y) inside its own slab.
All inputs are finite; a program needn't handle non-finite values. No bound on the sum of `bound_mask` on one device may be relied on, other than what follows from the above.
Results may differ from the reference program's by a relative error of at most 0.00017.
Values sent between devices are 32-bit elements; how exact they have to be, the bound alone decides.
A program may use at most 64 MiB of HBM per device.

```python
import math
import jax
import jax.numpy as jnp
from jax import lax

CZ = 8
NX = 32
NY = 256
STEPS = 2
CAPS = 32
CH = 25
RSLOT = 3
NZ = 128
SHOTS = 4
REC_SLOTS = 48


def draw_rec_live(key, part):
    slabs = REC_SLOTS // RSLOT
    groups = slabs // 4
    pattern = jnp.array([RSLOT, 1, 0, 0], dtype=jnp.int32)
    keys = jax.random.split(key, groups)
    orders = jax.vmap(lambda single: jax.random.permutation(single, 4))(keys)
    counts = pattern[orders].reshape(-1)
    slots = jnp.arange(RSLOT, dtype=jnp.int32)[None, :]
    return (slots < counts[:, None]).astype(jnp.int32).reshape(-1)


def draw_rec_cells(key, part):
    first, second, third = jax.random.split(jax.random.fold_in(key, 7), 3)
    corner_z = jax.random.randint(first, (REC_SLOTS, 1), 0, CZ - 1)
    corner_x = jax.random.randint(second, (REC_SLOTS, 1), 0, NX - 3)
    corner_y = jax.random.randint(third, (REC_SLOTS, 1), 0, NY - 3)
    corner_z = corner_z.at[0, 0].set(CZ - 2).at[1, 0].set(0)
    corner_x = corner_x.at[0, 0].set(NX - 4).at[1, 0].set(0)
    corner_y = corner_y.at[0, 0].set(NY - 4).at[1, 0].set(0)
    offsets = jnp.arange(32, dtype=jnp.int32)[None, :]
    step_z = offsets // 16
    step_x = offsets // 4 % 4
    step_y = offsets % 4
    flat = (corner_z + step_z) * NX * NY + (corner_x + step_x) * NY + (corner_y + step_y)
    return flat.astype(jnp.int32)


def with_ends(result, rng, smallest, high):
    longest = result.shape.index(max(result.shape))
    spots = []
    for shift in (0, 1):
        where = [jax.random.randint(jax.random.fold_in(rng, axis), (), 0, length) for axis, length in enumerate(result.shape)]
        where[longest] = (where[longest] + shift) % result.shape[longest]
        spots.append(tuple(where))
    return result.at[spots[0]].set(smallest).at[spots[1]].set(high)


def steps_of(rng, dims, shards, smallest, top_value):
    def one(axis_at, shards_of):
        heights = jax.random.uniform(jax.random.fold_in(jax.random.fold_in(rng, 6), axis_at), (shards_of,), jnp.float32, smallest / len(shards), top_value / len(shards))
        return jnp.repeat(jnp.exp(heights), dims[axis_at] // shards_of).reshape((-1,) + (1,) * (len(dims) - axis_at - 1))

    level = one(*shards[0])
    for cut in shards[1:]:
        level = level * one(*cut)
    return level


def centred(stream_key, dims, scale, reach, shards=(), held_as=jnp.bfloat16):
    drawn = jax.random.normal(stream_key, dims, jnp.float32) * scale
    if len(shards) > 0:
        drawn = steps_of(stream_key, dims, shards, -0.22, 0.18) * drawn
    return jnp.clip(drawn, min=-reach, max=reach).astype(held_as)


def setup_inputs(seed: int = 0) -> dict:
    arg_keys = jax.random.split(jax.random.key(seed), 11)
    pressure_init = centred(arg_keys[0], (SHOTS, NZ, NX, NY), 1.0, 6.0, ((0, 2), (1, 16)), jnp.float32)
    adjoint_init = centred(arg_keys[1], (SHOTS, NZ, NX, NY), 0.1, 1.5, ((0, 2), (1, 16)), jnp.float32)
    density = jnp.clip(jnp.exp(math.log(2.0) - 1.3862944 * jax.random.uniform(arg_keys[2], (NZ, NX, NY), jnp.float32) ** steps_of(arg_keys[2], (NZ, NX, NY), ((0, 16),), -0.2, 0.2)), 0.5, 2.0)
    speed = jnp.clip(0.6 + 0.5 * jax.random.uniform(arg_keys[3], (NZ, NX, NY), jnp.float32) ** steps_of(arg_keys[3], (NZ, NX, NY), ((0, 16),), -0.2, 0.2), 0.6, 1.1)
    admittance = jnp.clip(jnp.exp(math.log(0.5) - 2.3025851 * jax.random.uniform(arg_keys[4], (NZ, NX, NY), jnp.float32) ** steps_of(arg_keys[4], (NZ, NX, NY), ((0, 16),), -0.2, 0.2)), 0.05, 0.5)
    bound_mask = with_ends((jax.random.randint(arg_keys[5], (NZ, NX, NY), 0, 2) < 1).astype(jnp.int32), jax.random.fold_in(arg_keys[5], 1), 0, 1)
    rec_cells = draw_rec_cells(jax.random.fold_in(arg_keys[10], 71), 0)
    rec_live = draw_rec_live(jax.random.fold_in(arg_keys[10], 71), 0)
    encoder = centred(arg_keys[8], (CAPS, CH), CAPS ** -0.5, 1.0, (), jnp.float32)
    target = centred(arg_keys[9], (REC_SLOTS, SHOTS, STEPS, CH), 1.0, 6.0, ((0, 16), (1, 2)), jnp.float32)
    return dict(pressure_init=pressure_init, adjoint_init=adjoint_init, density=density, speed=speed, admittance=admittance, bound_mask=bound_mask, rec_cells=rec_cells, rec_live=rec_live, encoder=encoder, target=target)


def rise(values, along):
    widths = [(0, 0)] * values.ndim
    widths[along] = (0, 1)
    padded = jnp.pad(values, widths)
    return lax.slice_in_dim(padded, 1, values.shape[along] + 1, axis=along) - values


def fall(values, along):
    widths = [(0, 0)] * values.ndim
    widths[along] = (1, 0)
    padded = jnp.pad(values, widths)
    return values - lax.slice_in_dim(padded, 0, values.shape[along], axis=along)


def reference(pressure_init, adjoint_init, density, speed, admittance, bound_mask, rec_cells, rec_live, encoder, target):
    wall = bound_mask.astype(jnp.float32)
    vel_coef = 0.5 / density
    pres_coef = 0.5 * density * speed * speed
    damping = 1.0 - admittance * wall
    shots = pressure_init.shape[0]
    slab_cells = CZ * NX * NY
    owner = jnp.arange(REC_SLOTS, dtype=jnp.int32) // RSLOT
    cells = (rec_cells + (owner * slab_cells)[:, None]).astype(jnp.int32)
    live = rec_live.astype(jnp.float32)[:, None, None]
    pressure = pressure_init
    flow_x = jnp.zeros_like(pressure)
    flow_y = jnp.zeros_like(pressure)
    flow_z = jnp.zeros_like(pressure)
    saved = []
    misfit = []
    records = []
    for moment in range(STEPS):
        flow_x = flow_x - vel_coef * rise(pressure, 2)
        flow_y = flow_y - vel_coef * rise(pressure, 3)
        flow_z = flow_z - vel_coef * rise(pressure, 1)
        before = pressure - pres_coef * (fall(flow_x, 2) + fall(flow_y, 3) + fall(flow_z, 1))
        pressure = before * damping
        saved.append(before)
        sampled = pressure.reshape(shots, -1)[:, cells]
        encoded = jnp.einsum("src,ck->rsk", sampled, encoder, precision=lax.Precision.HIGHEST) * live
        records.append(encoded)
        misfit.append(encoded - target[:, :, moment, :] * live)
    recording = jnp.stack(records, axis=2)
    adjoint = adjoint_init
    back_x = jnp.zeros_like(adjoint)
    back_y = jnp.zeros_like(adjoint)
    back_z = jnp.zeros_like(adjoint)
    gradient = jnp.zeros(density.shape, jnp.float32)
    for moment in reversed(range(STEPS)):
        sources = jnp.einsum("rsk,ck->src", misfit[moment], encoder, precision=lax.Precision.HIGHEST)
        flat = adjoint.reshape(shots, -1).at[:, cells.reshape(-1)].add(sources.reshape(shots, -1))
        adjoint = flat.reshape(adjoint_init.shape)
        gradient = gradient - wall * jnp.sum(saved[moment] * adjoint, axis=0)
        if moment > 0:
            scaled = adjoint * damping
            weighted = pres_coef * scaled
            back_x = back_x - rise(weighted, 2)
            back_y = back_y - rise(weighted, 3)
            back_z = back_z - rise(weighted, 1)
            adjoint = scaled - (fall(vel_coef * back_x, 2) + fall(vel_coef * back_y, 3) + fall(vel_coef * back_z, 1))
    return recording, gradient
```

```python
import functools

import jax
import jax.numpy as jnp
from jax import lax
from jax.experimental import pallas as pl
from jax.experimental.pallas import tpu as pltpu
from jax.sharding import PartitionSpec as P

MESH = pl.DeviceIdType.MESH
F32 = jnp.float32


def split(value):
    high = value.astype(jnp.bfloat16)
    return high, (value - high.astype(F32)).astype(jnp.bfloat16)


def kernel(
    slabs,
    group,
    steps,
    slots,
    pressure_hbm,
    adjoint_hbm,
    density_hbm,
    speed_hbm,
    admittance_hbm,
    mask_hbm,
    cells_hbm,
    encoder_hbm,
    aux_hbm,
    record_hbm,
    grad_hbm,
    fields,
    weights,
    density,
    vel,
    pres,
    damp,
    mask,
    adjoint,
    before,
    after,
    placed,
    grads,
    total,
    cells,
    encoder,
    aux,
    record,
    load_sem,
    store_sem,
    send_sem,
    recv_sem,
    gsend_sem,
    grecv_sem,
):
    shots, depth, width_x, width_y = pressure_hbm.shape
    me = lax.axis_index("slab")
    mine = lax.axis_index("shot")
    has_below = me > 0
    has_above = me < slabs - 1

    inner = pl.ds(1, depth)
    pairs = [
        (density_hbm, density.at[inner]),
        (speed_hbm, pres),
        (admittance_hbm, damp),
        (mask_hbm, mask),
        (pressure_hbm, fields.at[0, :, inner]),
        (cells_hbm, cells),
        (encoder_hbm, encoder),
        (aux_hbm, aux),
        (adjoint_hbm, adjoint),
    ]
    loads = [pltpu.make_async_copy(a, b, load_sem.at[i]) for i, (a, b) in enumerate(pairs)]
    for load in loads:
        load.start()

    barrier = pltpu.get_barrier_semaphore()

    @pl.when(has_below)
    def _():
        pl.semaphore_signal(barrier, inc=1, device_id={"slab": me - 1}, device_id_type=MESH)

    @pl.when(has_above)
    def _():
        pl.semaphore_signal(barrier, inc=1, device_id={"slab": me + 1}, device_id_type=MESH)

    for j in range(1, group):
        pl.semaphore_signal(
            barrier, inc=1, device_id={"shot": lax.rem(mine + j, group)}, device_id_type=MESH
        )

    def halo(k, source, target, first, last):
        down = pltpu.make_async_remote_copy(
            src_ref=source.at[:, pl.ds(first, 1)],
            dst_ref=target.at[:, pl.ds(depth + 1, 1)],
            send_sem=send_sem.at[k, 0],
            recv_sem=recv_sem.at[k, 0],
            device_id={"slab": me - 1},
            device_id_type=MESH,
        )
        up = pltpu.make_async_remote_copy(
            src_ref=source.at[:, pl.ds(last, 1)],
            dst_ref=target.at[:, pl.ds(0, 1)],
            send_sem=send_sem.at[k, 1],
            recv_sem=recv_sem.at[k, 1],
            device_id={"slab": me + 1},
            device_id_type=MESH,
        )
        return down, up

    def start(pair):
        down, up = pair

        @pl.when(has_below)
        def _():
            down.start()

        @pl.when(has_above)
        def _():
            up.start()

    def arrive(pair):
        down, up = pair

        @pl.when(has_above)
        def _():
            down.wait_recv()

        @pl.when(has_below)
        def _():
            up.wait_recv()

    def sent(pair):
        down, up = pair

        @pl.when(has_below)
        def _():
            down.wait_send()

        @pl.when(has_above)
        def _():
            up.wait_send()

    rounds = [halo(0, pressure_hbm, fields.at[0], 0, depth - 1)]
    rounds += [halo(n, fields.at[n], fields.at[n], 1, depth) for n in range(1, steps)]
    rounds += [halo(steps + k, weights.at[k], weights.at[k], 1, depth) for k in range(steps - 1)]
    density_up = pltpu.make_async_remote_copy(
        src_ref=density_hbm.at[pl.ds(depth - 1, 1)],
        dst_ref=density.at[pl.ds(0, 1)],
        send_sem=send_sem.at[0, 2],
        recv_sem=recv_sem.at[0, 2],
        device_id={"slab": me + 1},
        device_id_type=MESH,
    )

    pl.semaphore_wait(
        barrier, has_below.astype(jnp.int32) + has_above.astype(jnp.int32) + (group - 1)
    )
    start(rounds[0])

    @pl.when(has_above)
    def _():
        density_up.start()

    zero = jnp.zeros((shots, width_x, width_y), F32)

    @pl.when(jnp.logical_not(has_below))
    def _():
        vel[0] = jnp.zeros((width_x, width_y), F32)
        for n in range(steps):
            fields[n, :, 0] = zero
        for k in range(steps - 1):
            weights[k, :, 0] = zero

    @pl.when(jnp.logical_not(has_above))
    def _():
        for n in range(steps):
            fields[n, :, depth + 1] = zero
        for k in range(steps - 1):
            weights[k, :, depth + 1] = zero

    rows = lax.broadcasted_iota(jnp.int32, (width_x, width_y), 0)
    cols = lax.broadcasted_iota(jnp.int32, (width_x, width_y), 1)

    def next_x(v):
        return jnp.where(rows == width_x - 1, 0.0, pltpu.roll(v, width_x - 1, 0))

    def next_y(v):
        return jnp.where(cols == width_y - 1, 0.0, pltpu.roll(v, width_y - 1, 1))

    def prev_x(v):
        return jnp.where(rows == 0, 0.0, pltpu.roll(v, 1, 0))

    def prev_y(v):
        return jnp.where(cols == 0, 0.0, pltpu.roll(v, 1, 1))

    def spread(ref, n, s, z):
        q = ref[n, s, z]
        v = vel[z]
        along_z = v * (ref[n, s, z + 1] - q) - vel[z - 1] * (q - ref[n, s, z - 1])
        along_x = v * (next_x(q) - q)
        along_y = v * (next_y(q) - q)
        return along_z + (along_x - prev_x(along_x)) + (along_y - prev_y(along_y))

    def forward(n, z):
        for s in range(shots):
            base = fields[0, s, z] if n == 0 else after[n - 1, s, z - 1]
            value = base + pres[z - 1] * spread(fields, n, s, z)
            before[n, s, z - 1] = value
            value = value * damp[z - 1]
            after[n, s, z - 1] = value
            if n + 1 < steps:
                fields[n + 1, s, z] = fields[n, s, z] + value

    def backward(n, z):
        k = steps - 1 - n
        part = jnp.zeros((width_x, width_y), F32)
        for s in range(shots):
            value = adjoint[s, z - 1] + placed[n, s, z - 1]
            if k > 0:
                value = value + spread(weights, k - 1, s, z)
            part = part + before[n, s, z - 1] * value
            if n > 0:
                scaled = value * damp[z - 1]
                adjoint[s, z - 1] = scaled
                weighted = pres[z - 1] * scaled
                if k > 0:
                    weighted = weighted + weights[k - 1, s, z]
                weights[k, s, z] = weighted
        if k > 0:
            part = grads[mine, z - 1] + part
        grads[mine, z - 1] = part

    def over(low, high, step):
        def run(z, carry):
            step(z)
            return carry

        lax.fori_loop(low, high, run, 0)

    edges = (1, depth)
    middle = tuple(range(2, depth))

    for load in loads[:4]:
        load.wait()

    def coefficients(z):
        rho = density[z]
        vel[z] = 0.5 / rho
        c = pres[z - 1]
        pres[z - 1] = 0.5 * rho * c * c
        damp[z - 1] = 1.0 - damp[z - 1] * mask[z - 1].astype(F32)

    over(1, depth + 1, coefficients)
    for load in loads[4:8]:
        load.wait()

    caps = encoder.shape[0]
    count = slots * caps
    flat = cells[...]
    plane_at = flat // width_y
    col_at = flat - plane_at * width_y
    pick_col = jnp.where(
        lax.broadcasted_iota(jnp.int32, (width_y, count), 0) == col_at, 1.0, 0.0
    ).astype(jnp.bfloat16)
    band = lax.broadcasted_iota(jnp.int32, (width_x, count), 0)

    def pick_plane(z):
        return band + (z - 1) * width_x == plane_at

    pad = record.shape[1]
    row_of = lax.broadcasted_iota(jnp.int32, (pad, count), 0)
    slot_of = lax.broadcasted_iota(jnp.int32, (pad, count), 1) // caps
    owns = [row_of == slot_of * shots + s for s in range(shots)]
    filters = jnp.concatenate([encoder[...]] * slots, axis=0)

    def sample(n, planes):
        highs, lows = [], []
        for s in range(shots):
            for z in planes:
                high, low = split(after[n, s, z - 1])
                highs.append(high)
                lows.append(low)
        got = jnp.dot(
            jnp.concatenate(highs + lows, axis=0), pick_col, preferred_element_type=F32
        )
        found = []
        at = 0
        half = len(highs) * width_x
        for s in range(shots):
            part = jnp.zeros((width_x, count), F32)
            for z in planes:
                value = got[at : at + width_x] + got[half + at : half + at + width_x]
                part = part + jnp.where(pick_plane(z), value, 0.0)
                at += width_x
            found.append(jnp.sum(part, axis=0, keepdims=True))
        return found

    def encode(n, found):
        table = jnp.zeros((pad, count), F32)
        for s in range(shots):
            table = jnp.where(owns[s], found[s], table)
        encoded = (
            jnp.dot(table, filters, precision=lax.Precision.HIGHEST, preferred_element_type=F32)
            * aux[steps]
        )
        record[n] = encoded
        wide = lax.dot_general(
            encoded - aux[n],
            filters,
            (((1,), (1,)), ((), ())),
            precision=lax.Precision.HIGHEST,
            preferred_element_type=F32,
        )
        return [
            jnp.sum(jnp.where(owns[s], wide, 0.0), axis=0, keepdims=True) for s in range(shots)
        ]

    def place(n, sources, planes):
        highs, lows = [], []
        for s in range(shots):
            high, low = split(sources[s])
            high, low = high.astype(F32), low.astype(F32)
            for z in planes:
                pick = pick_plane(z)
                highs.append(jnp.where(pick, high, 0.0).astype(jnp.bfloat16))
                lows.append(jnp.where(pick, low, 0.0).astype(jnp.bfloat16))
        put = lax.dot_general(
            jnp.concatenate(highs + lows, axis=0),
            pick_col,
            (((1,), (1,)), ((), ())),
            preferred_element_type=F32,
        )
        at = 0
        half = len(highs) * width_x
        for s in range(shots):
            for z in planes:
                placed[n, s, z - 1] = put[at : at + width_x] + put[half + at : half + at + width_x]
                at += width_x

    found = [None] * steps
    sources = [None] * steps
    for n in range(steps):
        over(2, depth, functools.partial(forward, n))
        if n > 0:
            found[n - 1] = sample(n - 1, middle + edges)
            sources[n - 1] = encode(n - 1, found[n - 1])
            place(n - 1, sources[n - 1], middle + edges)
        if n == steps - 1:
            inside = sample(n, middle)
        arrive(rounds[n])
        if n == 0:

            @pl.when(has_below)
            def _():
                density_up.wait_recv()
                vel[0] = 0.5 / density[0]

        for z in edges:
            forward(n, z)
        if n + 1 < steps:
            start(rounds[n + 1])

    last = steps - 1
    outside = sample(last, edges)
    sources[last] = encode(last, [a + b for a, b in zip(inside, outside)])
    loads[8].wait()
    record_store = pltpu.make_async_copy(record, record_hbm, store_sem.at[0])
    record_store.start()

    def share(k, low, size):
        planes = pl.ds(low, size)
        copies = []
        for j in range(1, group):
            copies.append(
                pltpu.make_async_remote_copy(
                    src_ref=grads.at[mine, planes],
                    dst_ref=grads.at[mine, planes],
                    send_sem=gsend_sem.at[k, j - 1],
                    recv_sem=grecv_sem.at[k, j - 1],
                    device_id={"shot": lax.rem(mine + j, group)},
                    device_id_type=MESH,
                )
            )
        return copies

    parts = [(1, depth - 2), (0, 1), (depth - 1, 1)]
    shares = [share(k, low, size) for k, (low, size) in enumerate(parts)]

    for n in reversed(range(steps)):
        k = last - n
        if k == 0:
            place(n, sources[n], edges)
            for z in edges:
                backward(n, z)
            if n > 0:
                start(rounds[steps])
            place(n, sources[n], middle)
            over(2, depth, functools.partial(backward, n))
        else:
            over(2, depth, functools.partial(backward, n))
            if n == 0:
                for copy in shares[0]:
                    copy.start()
            arrive(rounds[steps + k - 1])
            for z in edges:
                backward(n, z)
            if n > 0:
                start(rounds[steps + k])
    if steps == 1:
        for copy in shares[0]:
            copy.start()
    for copy in shares[1] + shares[2]:
        copy.start()

    stores = []
    for k, (low, size) in enumerate(parts):
        for copy in shares[k]:
            copy.wait_recv()
        planes = pl.ds(low, size)
        value = grads[0, planes]
        for t in range(1, group):
            value = value + grads[t, planes]
        total[planes] = value
        store = pltpu.make_async_copy(total.at[planes], grad_hbm.at[planes], store_sem.at[1 + k])
        store.start()
        stores.append(store)

    for pair in rounds:
        sent(pair)

    @pl.when(has_above)
    def _():
        density_up.wait_send()

    for copies in shares:
        for copy in copies:
            copy.wait_send()
    record_store.wait()
    for store in stores:
        store.wait()


def solution(mesh):
    slabs, group = mesh.shape["slab"], mesh.shape["shot"]

    def body(
        pressure_init,
        adjoint_init,
        density,
        speed,
        admittance,
        bound_mask,
        rec_cells,
        rec_live,
        encoder,
        target,
    ):
        shots, depth, width_x, width_y = pressure_init.shape
        slots, caps = rec_cells.shape
        steps, channels = target.shape[2], target.shape[3]
        count = slots * shots
        pad = -(-count // 8) * 8
        live = rec_live.astype(F32)[:, None, None, None]
        signals = jnp.transpose(target * live, (2, 0, 1, 3)).reshape(steps, count, channels)
        lives = jnp.broadcast_to(live, (slots, shots, 1, channels)).reshape(1, count, channels)
        aux = jnp.pad(
            jnp.concatenate([signals, lives], axis=0), ((0, 0), (0, pad - count), (0, 0))
        )
        plane = (depth, width_x, width_y)
        padded = (shots, depth + 2, width_x, width_y)
        any_spec = pl.BlockSpec(memory_space=pl.ANY)
        record, total = pl.pallas_call(
            functools.partial(kernel, slabs, group, steps, slots),
            out_shape=(
                jax.ShapeDtypeStruct((steps, pad, channels), F32),
                jax.ShapeDtypeStruct(plane, F32),
            ),
            in_specs=[any_spec] * 9,
            out_specs=(any_spec, any_spec),
            scratch_shapes=[
                pltpu.VMEM((steps,) + padded, F32),
                pltpu.VMEM((max(steps - 1, 1),) + padded, F32),
                pltpu.VMEM((depth + 1, width_x, width_y), F32),
                pltpu.VMEM((depth + 1, width_x, width_y), F32),
                pltpu.VMEM(plane, F32),
                pltpu.VMEM(plane, F32),
                pltpu.VMEM(plane, jnp.int32),
                pltpu.VMEM((shots,) + plane, F32),
                pltpu.VMEM((steps, shots) + plane, F32),
                pltpu.VMEM((steps, shots) + plane, F32),
                pltpu.VMEM((steps, shots) + plane, F32),
                pltpu.VMEM((group,) + plane, F32),
                pltpu.VMEM(plane, F32),
                pltpu.VMEM((1, slots * caps), jnp.int32),
                pltpu.VMEM((caps, channels), F32),
                pltpu.VMEM((steps + 1, pad, channels), F32),
                pltpu.VMEM((steps, pad, channels), F32),
                pltpu.SemaphoreType.DMA((9,)),
                pltpu.SemaphoreType.DMA((4,)),
                pltpu.SemaphoreType.DMA((2 * steps, 3)),
                pltpu.SemaphoreType.DMA((2 * steps, 3)),
                pltpu.SemaphoreType.DMA((3, max(group - 1, 1))),
                pltpu.SemaphoreType.DMA((3, max(group - 1, 1))),
            ],
            compiler_params=pltpu.CompilerParams(
                collective_id=0, has_side_effects=True, vmem_limit_bytes=40 * 1024 * 1024
            ),
        )(
            pressure_init,
            adjoint_init,
            density,
            speed,
            admittance,
            bound_mask,
            rec_cells.reshape(1, slots * caps),
            encoder,
            aux,
        )
        recording = jnp.transpose(
            record[:, :count].reshape(steps, slots, shots, channels), (1, 2, 0, 3)
        )
        gradient = -(bound_mask.astype(F32) * total)
        return recording, gradient

    placed = (
        P("shot", "slab", None, None),
        P("shot", "slab", None, None),
        P("slab", None, None),
        P("slab", None, None),
        P("slab", None, None),
        P("slab", None, None),
        P("slab", None),
        P("slab"),
        P(),
        P("slab", "shot", None, None),
    )
    return jax.shard_map(
        body,
        mesh=mesh,
        in_specs=placed,
        out_specs=(P("slab", "shot", None, None), P("slab", None, None)),
        check_vma=False,
    )
```

```python
import functools

import jax
import jax.numpy as jnp
from jax import lax
from jax.experimental import pallas as pl
from jax.experimental.pallas import tpu as pltpu
from jax.sharding import PartitionSpec as P

MESH = pl.DeviceIdType.MESH
F32 = jnp.float32


def split(value):
    high = value.astype(jnp.bfloat16)
    return high, (value - high.astype(F32)).astype(jnp.bfloat16)


def kernel(
    slabs,
    group,
    steps,
    slots,
    pressure_hbm,
    adjoint_hbm,
    density_hbm,
    speed_hbm,
    admittance_hbm,
    mask_hbm,
    cells_hbm,
    live_hbm,
    encoder_hbm,
    target_hbm,
    record_hbm,
    grad_hbm,
    fields,
    weights,
    density,
    vel,
    pres,
    damp,
    mask,
    adjoint,
    before,
    after,
    placed,
    grads,
    total,
    cells,
    live,
    encoder,
    target,
    record,
    load_sem,
    store_sem,
    send_sem,
    recv_sem,
    gsend_sem,
    grecv_sem,
):
    shots, depth, width_x, width_y = pressure_hbm.shape
    me = lax.axis_index("slab")
    mine = lax.axis_index("shot")
    has_below = me > 0
    has_above = me < slabs - 1

    inner = pl.ds(1, depth)
    pairs = [
        (density_hbm, density.at[inner]),
        (speed_hbm, pres),
        (admittance_hbm, damp),
        (mask_hbm, mask),
        (pressure_hbm, fields.at[0, :, inner]),
        (cells_hbm, cells),
        (live_hbm, live),
        (encoder_hbm, encoder),
        (target_hbm, target),
        (adjoint_hbm, adjoint),
    ]
    loads = [pltpu.make_async_copy(a, b, load_sem.at[i]) for i, (a, b) in enumerate(pairs)]
    for load in loads:
        load.start()

    barrier = pltpu.get_barrier_semaphore()

    @pl.when(has_below)
    def _():
        pl.semaphore_signal(barrier, inc=1, device_id={"slab": me - 1}, device_id_type=MESH)

    @pl.when(has_above)
    def _():
        pl.semaphore_signal(barrier, inc=1, device_id={"slab": me + 1}, device_id_type=MESH)

    for j in range(1, group):
        pl.semaphore_signal(
            barrier, inc=1, device_id={"shot": lax.rem(mine + j, group)}, device_id_type=MESH
        )

    def halo(k, s, source, into, first, last):
        down = pltpu.make_async_remote_copy(
            src_ref=source.at[s, pl.ds(first, 1)],
            dst_ref=into.at[s, pl.ds(depth + 1, 1)],
            send_sem=send_sem.at[k, s, 0],
            recv_sem=recv_sem.at[k, s, 0],
            device_id={"slab": me - 1},
            device_id_type=MESH,
        )
        up = pltpu.make_async_remote_copy(
            src_ref=source.at[s, pl.ds(last, 1)],
            dst_ref=into.at[s, pl.ds(0, 1)],
            send_sem=send_sem.at[k, s, 1],
            recv_sem=recv_sem.at[k, s, 1],
            device_id={"slab": me + 1},
            device_id_type=MESH,
        )
        return down, up

    def start(pair):
        down, up = pair

        @pl.when(has_below)
        def _():
            down.start()

        @pl.when(has_above)
        def _():
            up.start()

    def arrive(pair):
        down, up = pair

        @pl.when(has_above)
        def _():
            down.wait_recv()

        @pl.when(has_below)
        def _():
            up.wait_recv()

    def sent(pair):
        down, up = pair

        @pl.when(has_below)
        def _():
            down.wait_send()

        @pl.when(has_above)
        def _():
            up.wait_send()

    each = range(shots)
    rounds = [[halo(0, s, pressure_hbm, fields.at[0], 0, depth - 1) for s in each]]
    for n in range(1, steps):
        rounds.append([halo(n, s, fields.at[n], fields.at[n], 1, depth) for s in each])
    for k in range(steps - 1):
        rounds.append(
            [halo(steps + k, s, weights.at[k], weights.at[k], 1, depth) for s in each]
        )
    density_up = pltpu.make_async_remote_copy(
        src_ref=density_hbm.at[pl.ds(depth - 1, 1)],
        dst_ref=density.at[pl.ds(0, 1)],
        send_sem=send_sem.at[0, 0, 2],
        recv_sem=recv_sem.at[0, 0, 2],
        device_id={"slab": me + 1},
        device_id_type=MESH,
    )

    pl.semaphore_wait(
        barrier, has_below.astype(jnp.int32) + has_above.astype(jnp.int32) + (group - 1)
    )

    @pl.when(has_above)
    def _():
        density_up.start()

    for s in each:
        start(rounds[0][s])

    zero = jnp.zeros((shots, width_x, width_y), F32)

    @pl.when(jnp.logical_not(has_below))
    def _():
        vel[0] = jnp.zeros((width_x, width_y), F32)
        for n in range(steps):
            fields[n, :, 0] = zero
        for k in range(steps - 1):
            weights[k, :, 0] = zero

    @pl.when(jnp.logical_not(has_above))
    def _():
        for n in range(steps):
            fields[n, :, depth + 1] = zero
        for k in range(steps - 1):
            weights[k, :, depth + 1] = zero

    rows = lax.broadcasted_iota(jnp.int32, (width_x, width_y), 0)
    cols = lax.broadcasted_iota(jnp.int32, (width_x, width_y), 1)

    def next_x(v):
        return jnp.where(rows == width_x - 1, 0.0, pltpu.roll(v, width_x - 1, 0))

    def next_y(v):
        return jnp.where(cols == width_y - 1, 0.0, pltpu.roll(v, width_y - 1, 1))

    def prev_x(v):
        return jnp.where(rows == 0, 0.0, pltpu.roll(v, 1, 0))

    def prev_y(v):
        return jnp.where(cols == 0, 0.0, pltpu.roll(v, 1, 1))

    def spread(ref, n, s, z):
        q = ref[n, s, z]
        v = vel[z]
        along_z = v * (ref[n, s, z + 1] - q) - vel[z - 1] * (q - ref[n, s, z - 1])
        along_x = v * (next_x(q) - q)
        along_y = v * (next_y(q) - q)
        return along_z + (along_x - prev_x(along_x)) + (along_y - prev_y(along_y))

    def forward(n, which, z):
        for s in which:
            base = fields[0, s, z] if n == 0 else after[n - 1, s, z - 1]
            value = base + pres[z - 1] * spread(fields, n, s, z)
            before[n, s, z - 1] = value
            value = value * damp[z - 1]
            after[n, s, z - 1] = value
            if n + 1 < steps:
                fields[n + 1, s, z] = fields[n, s, z] + value

    def backward(n, which, z):
        k = steps - 1 - n
        part = None if k == 0 and 0 in which else grads[mine, z - 1]
        for s in which:
            value = adjoint[s, z - 1] + placed[n, s, z - 1]
            if k > 0:
                value = value + spread(weights, k - 1, s, z)
            term = before[n, s, z - 1] * value
            part = term if part is None else part + term
            if n > 0:
                scaled = value * damp[z - 1]
                adjoint[s, z - 1] = scaled
                weighted = pres[z - 1] * scaled
                if k > 0:
                    weighted = weighted + weights[k - 1, s, z]
                weights[k, s, z] = weighted
        grads[mine, z - 1] = part

    def over(low, high, step):
        size = max(g for g in (1, 2, 3) if (high - low) % g == 0)

        def run(i, carry):
            for j in range(size):
                step(low + i * size + j)
            return carry

        lax.fori_loop(0, (high - low) // size, run, 0)

    edges = (1, depth)
    middle = tuple(range(2, depth))

    for load in loads[:4]:
        load.wait()

    def coefficients(z):
        rho = density[z]
        vel[z] = 0.5 / rho
        c = pres[z - 1]
        pres[z - 1] = 0.5 * rho * c * c
        damp[z - 1] = 1.0 - damp[z - 1] * mask[z - 1].astype(F32)

    over(1, depth + 1, coefficients)
    for load in loads[4:9]:
        load.wait()

    caps, channels = encoder.shape
    count = slots * caps
    lanes = -(-count // 128) * 128
    spare = lanes - count
    flat = [cells[pl.ds(r, 1), :] for r in range(slots)]
    if spare:
        flat.append(jnp.full((1, spare), -1, jnp.int32))
    flat = jnp.concatenate(flat, axis=1)
    plane_at = flat // width_y
    col_at = flat - plane_at * width_y
    pick_col = jnp.where(
        lax.broadcasted_iota(jnp.int32, (width_y, lanes), 0) == col_at, 1.0, 0.0
    ).astype(jnp.bfloat16)
    read_col = jnp.concatenate([pick_col, pick_col], axis=0)
    write_col = jnp.concatenate([pick_col, pick_col], axis=1)
    plane_twice = jnp.concatenate([plane_at, plane_at], axis=1)
    band = lax.broadcasted_iota(jnp.int32, (width_x, lanes), 0)
    band_twice = lax.broadcasted_iota(jnp.int32, (width_x, 2 * lanes), 0)

    pad = -(-slots * shots // 8) * 8
    slot_of = lax.broadcasted_iota(jnp.int32, (1, lanes), 1) // caps
    row_of = lax.broadcasted_iota(jnp.int32, (pad, lanes), 0)
    owns = [row_of == slot_of * shots + s for s in range(shots)]
    row_at = lax.broadcasted_iota(jnp.int32, (pad, channels), 0)
    live_row = jnp.zeros((pad, channels), F32)
    live_lane = jnp.zeros((1, lanes), F32)
    for r in range(slots):
        alive = live[r].astype(F32)
        live_row = jnp.where(row_at // shots == r, alive, live_row)
        live_lane = jnp.where(slot_of == r, alive, live_lane)
    filters = [encoder[...]] * slots
    if spare:
        filters.append(jnp.zeros((spare, channels), F32))
    filters = jnp.concatenate(filters, axis=0)

    def exact(a, b, contract):
        return lax.dot_general(
            a,
            b,
            (contract, ((), ())),
            precision=lax.Precision.HIGHEST,
            preferred_element_type=F32,
        )

    gram = exact(filters, filters, ((1,), (1,)))
    same = lax.broadcasted_iota(jnp.int32, (lanes, lanes), 0) // caps == slot_of
    gram_high, gram_low = split(jnp.where(same, gram, 0.0))
    gram = jnp.concatenate([gram_high, gram_high, gram_low], axis=0)

    goals = []
    for n in range(steps):
        signal = jnp.zeros((pad, channels), F32)
        for r in range(slots):
            for s in range(shots):
                signal = jnp.where(row_at == r * shots + s, target[r, s, pl.ds(n, 1), :], signal)
        wide = exact(signal * live_row, filters, ((1,), (1,)))
        goals.append(
            [
                jnp.sum(jnp.where(owns[s], wide, 0.0), axis=0, keepdims=True)
                for s in range(shots)
            ]
        )

    def sample(n, s, planes):
        values = jnp.concatenate([after[n, s, z - 1] for z in planes], axis=0)
        got = jnp.dot(
            jnp.concatenate(split(values), axis=1), read_col, preferred_element_type=F32
        )
        part = jnp.zeros((width_x, lanes), F32)
        for i, z in enumerate(planes):
            pick = band + (z - 1) * width_x == plane_at
            part = part + jnp.where(pick, got[i * width_x : (i + 1) * width_x], 0.0)
        return jnp.sum(part, axis=0, keepdims=True)

    def encode(n, found):
        table = jnp.zeros((pad, lanes), F32)
        for s in range(shots):
            table = jnp.where(owns[s], found[s], table)
        encoded = exact(table, filters, ((1,), (0,))) * live_row
        for r in range(slots):
            for s in range(shots):
                i = r * shots + s
                record[r, s, pl.ds(n, 1), :] = encoded[i : i + 1]

    def source(n, s, found):
        high, low = split(jnp.broadcast_to(found, (16, lanes)))
        wide = jnp.dot(
            jnp.concatenate([high, low, high], axis=1), gram, preferred_element_type=F32
        )
        return wide[0:1] * live_lane - goals[n][s]

    def place(n, s, value, planes):
        high, low = split(value)
        both = jnp.concatenate([high.astype(F32), low.astype(F32)], axis=1)
        spots = []
        for z in planes:
            pick = band_twice + (z - 1) * width_x == plane_twice
            spots.append(jnp.where(pick, both, 0.0).astype(jnp.bfloat16))
        put = lax.dot_general(
            jnp.concatenate(spots, axis=0),
            write_col,
            (((1,), (1,)), ((), ())),
            preferred_element_type=F32,
        )
        for i, z in enumerate(planes):
            placed[n, s, z - 1] = put[i * width_x : (i + 1) * width_x]

    last = steps - 1
    for n in range(steps):
        over(2, depth, functools.partial(forward, n, each))
        if n == last:
            found = [sample(n, s, middle) for s in each]
            loads[9].wait()
        if n == 0:

            @pl.when(has_below)
            def _():
                density_up.wait_recv()
                vel[0] = 0.5 / density[0]

        sources = []
        for s in each:
            arrive(rounds[n][s])
            for z in edges:
                forward(n, (s,), z)
            if n < last:
                start(rounds[n + 1][s])
            else:
                found[s] = found[s] + sample(n, s, edges)
                sources.append(source(n, s, found[s]))
                place(n, s, sources[s], edges)
                for z in edges:
                    backward(n, (s,), z)
                if n > 0:
                    start(rounds[steps][s])

    record_store = pltpu.make_async_copy(record, record_hbm, store_sem.at[0])

    def share(k, low, size):
        planes = pl.ds(low, size)
        copies = []
        for j in range(1, group):
            copies.append(
                pltpu.make_async_remote_copy(
                    src_ref=grads.at[mine, planes],
                    dst_ref=grads.at[mine, planes],
                    send_sem=gsend_sem.at[k, j - 1],
                    recv_sem=grecv_sem.at[k, j - 1],
                    device_id={"shot": lax.rem(mine + j, group)},
                    device_id_type=MESH,
                )
            )
        return copies

    parts = [(1, depth - 2), (0, 1), (depth - 1, 1)]
    shares = [share(k, low, size) for k, (low, size) in enumerate(parts)]

    for s in each:
        place(last, s, sources[s], middle)
    over(2, depth, functools.partial(backward, last, each))
    for n in reversed(range(last)):
        k = last - n
        old = [sample(n, s, middle + edges) for s in each]
        for s in each:
            place(n, s, source(n, s, old[s]), middle + edges)
        over(2, depth, functools.partial(backward, n, each))
        if n == 0:
            for copy in shares[0]:
                copy.start()
        encode(n, old)
        if n == 0:
            encode(last, found)
            record_store.start()
        for s in each:
            arrive(rounds[steps + k - 1][s])
            for z in edges:
                backward(n, (s,), z)
            if n > 0:
                start(rounds[steps + k][s])
    if steps == 1:
        encode(last, found)
        record_store.start()
        for copy in shares[0]:
            copy.start()
    for copy in shares[1] + shares[2]:
        copy.start()

    stores = []
    for k, (low, size) in enumerate(parts):
        for copy in shares[k]:
            copy.wait_recv()
        planes = pl.ds(low, size)
        value = grads[0, planes]
        for t in range(1, group):
            value = value + grads[t, planes]
        total[planes] = value
        store = pltpu.make_async_copy(total.at[planes], grad_hbm.at[planes], store_sem.at[1 + k])
        store.start()
        stores.append(store)

    for pairs in rounds:
        for pair in pairs:
            sent(pair)

    @pl.when(has_above)
    def _():
        density_up.wait_send()

    for copies in shares:
        for copy in copies:
            copy.wait_send()
    record_store.wait()
    for store in stores:
        store.wait()


def solution(mesh):
    slabs, group = mesh.shape["slab"], mesh.shape["shot"]

    def body(
        pressure_init,
        adjoint_init,
        density,
        speed,
        admittance,
        bound_mask,
        rec_cells,
        rec_live,
        encoder,
        target,
    ):
        shots, depth, width_x, width_y = pressure_init.shape
        slots, caps = rec_cells.shape
        steps, channels = target.shape[2], target.shape[3]
        plane = (depth, width_x, width_y)
        padded = (shots, depth + 2, width_x, width_y)
        any_spec = pl.BlockSpec(memory_space=pl.ANY)
        hbm_spec = any_spec
        record, total = pl.pallas_call(
            functools.partial(kernel, slabs, group, steps, slots),
            out_shape=(
                jax.ShapeDtypeStruct(target.shape, F32),
                jax.ShapeDtypeStruct(plane, F32),
            ),
            in_specs=[hbm_spec] * 10,
            out_specs=(any_spec, any_spec),
            scratch_shapes=[
                pltpu.VMEM((steps,) + padded, F32),
                pltpu.VMEM((max(steps - 1, 1),) + padded, F32),
                pltpu.VMEM((depth + 1, width_x, width_y), F32),
                pltpu.VMEM((depth + 1, width_x, width_y), F32),
                pltpu.VMEM(plane, F32),
                pltpu.VMEM(plane, F32),
                pltpu.VMEM(plane, jnp.int32),
                pltpu.VMEM((shots,) + plane, F32),
                pltpu.VMEM((steps, shots) + plane, F32),
                pltpu.VMEM((steps, shots) + plane, F32),
                pltpu.VMEM((steps, shots) + plane, F32),
                pltpu.VMEM((group,) + plane, F32),
                pltpu.VMEM(plane, F32),
                pltpu.VMEM((slots, caps), jnp.int32),
                pltpu.SMEM((slots,), jnp.int32),
                pltpu.VMEM((caps, channels), F32),
                pltpu.VMEM(target.shape, F32),
                pltpu.VMEM(target.shape, F32),
                pltpu.SemaphoreType.DMA((10,)),
                pltpu.SemaphoreType.DMA((4,)),
                pltpu.SemaphoreType.DMA((2 * steps, shots, 3)),
                pltpu.SemaphoreType.DMA((2 * steps, shots, 3)),
                pltpu.SemaphoreType.DMA((3, max(group - 1, 1))),
                pltpu.SemaphoreType.DMA((3, max(group - 1, 1))),
            ],
            compiler_params=pltpu.CompilerParams(
                collective_id=0, has_side_effects=True, vmem_limit_bytes=62 * 1024 * 1024
            ),
        )(
            pressure_init,
            adjoint_init,
            density,
            speed,
            admittance,
            bound_mask,
            rec_cells,
            rec_live,
            encoder,
            target,
        )
        gradient = -(bound_mask.astype(F32) * total)
        return record, gradient

    placed = (
        P("shot", "slab", None, None),
        P("shot", "slab", None, None),
        P("slab", None, None),
        P("slab", None, None),
        P("slab", None, None),
        P("slab", None, None),
        P("slab", None),
        P("slab"),
        P(),
        P("slab", "shot", None, None),
    )
    return jax.shard_map(
        body,
        mesh=mesh,
        in_specs=placed,
        out_specs=(P("slab", "shot", None, None), P("slab", None, None)),
        check_vma=False,
    )
```

```python
import functools

import jax
import jax.numpy as jnp
from jax import lax
from jax.experimental import pallas as pl
from jax.experimental.pallas import tpu as pltpu
from jax.sharding import PartitionSpec as P

MESH = pl.DeviceIdType.MESH
F32 = jnp.float32


def split(value):
    high = value.astype(jnp.bfloat16)
    return high, (value - high.astype(F32)).astype(jnp.bfloat16)


def kernel(
    slabs,
    group,
    steps,
    slots,
    pressure_hbm,
    adjoint_hbm,
    density_hbm,
    speed_hbm,
    admittance_hbm,
    mask_hbm,
    cells_hbm,
    live_hbm,
    encoder_hbm,
    target_hbm,
    record,
    total,
    fields,
    weights,
    density,
    vel,
    next_x,
    prev_x,
    next_y,
    prev_y,
    centre,
    pres,
    damp,
    mask,
    adjoint,
    before,
    after,
    placed,
    grads,
    cells,
    live,
    encoder,
    target,
    load_sem,
    send_sem,
    recv_sem,
    gsend_sem,
    grecv_sem,
):
    shots, depth, width_x, width_y = pressure_hbm.shape
    me = lax.axis_index("slab")
    mine = lax.axis_index("shot")
    has_below = me > 0
    has_above = me < slabs - 1

    inner = pl.ds(1, depth)
    pairs = [
        (density_hbm, density.at[inner]),
        (speed_hbm, pres),
        (admittance_hbm, damp),
        (mask_hbm, mask),
        (pressure_hbm, fields.at[0, :, inner]),
        (cells_hbm, cells),
        (live_hbm, live),
        (encoder_hbm, encoder),
        (target_hbm, target),
        (adjoint_hbm, adjoint),
    ]
    loads = [pltpu.make_async_copy(a, b, load_sem.at[i]) for i, (a, b) in enumerate(pairs)]
    for load in loads:
        load.start()

    barrier = pltpu.get_barrier_semaphore()

    @pl.when(has_below)
    def _():
        pl.semaphore_signal(barrier, inc=1, device_id={"slab": me - 1}, device_id_type=MESH)

    @pl.when(has_above)
    def _():
        pl.semaphore_signal(barrier, inc=1, device_id={"slab": me + 1}, device_id_type=MESH)

    for j in range(1, group):
        pl.semaphore_signal(
            barrier, inc=1, device_id={"shot": lax.rem(mine + j, group)}, device_id_type=MESH
        )

    def halo(k, s, source, into, first, last):
        down = pltpu.make_async_remote_copy(
            src_ref=source.at[s, pl.ds(first, 1)],
            dst_ref=into.at[s, pl.ds(depth + 1, 1)],
            send_sem=send_sem.at[k, s, 0],
            recv_sem=recv_sem.at[k, s, 0],
            device_id={"slab": me - 1},
            device_id_type=MESH,
        )
        up = pltpu.make_async_remote_copy(
            src_ref=source.at[s, pl.ds(last, 1)],
            dst_ref=into.at[s, pl.ds(0, 1)],
            send_sem=send_sem.at[k, s, 1],
            recv_sem=recv_sem.at[k, s, 1],
            device_id={"slab": me + 1},
            device_id_type=MESH,
        )
        return down, up

    def start(pair):
        down, up = pair

        @pl.when(has_below)
        def _():
            down.start()

        @pl.when(has_above)
        def _():
            up.start()

    def arrive(pair):
        down, up = pair

        @pl.when(has_above)
        def _():
            down.wait_recv()

        @pl.when(has_below)
        def _():
            up.wait_recv()

    def sent(pair):
        down, up = pair

        @pl.when(has_below)
        def _():
            down.wait_send()

        @pl.when(has_above)
        def _():
            up.wait_send()

    each = range(shots)
    rounds = [[halo(0, s, pressure_hbm, fields.at[0], 0, depth - 1) for s in each]]
    for n in range(1, steps):
        rounds.append([halo(n, s, fields.at[n], fields.at[n], 1, depth) for s in each])
    for k in range(steps - 1):
        rounds.append(
            [halo(steps + k, s, weights.at[k], weights.at[k], 1, depth) for s in each]
        )
    density_up = pltpu.make_async_remote_copy(
        src_ref=density_hbm.at[pl.ds(depth - 1, 1)],
        dst_ref=density.at[pl.ds(0, 1)],
        send_sem=send_sem.at[0, 0, 2],
        recv_sem=recv_sem.at[0, 0, 2],
        device_id={"slab": me + 1},
        device_id_type=MESH,
    )

    pl.semaphore_wait(
        barrier, has_below.astype(jnp.int32) + has_above.astype(jnp.int32) + (group - 1)
    )

    @pl.when(has_above)
    def _():
        density_up.start()

    for s in each:
        start(rounds[0][s])

    zero = jnp.zeros((shots, width_x, width_y), F32)

    @pl.when(jnp.logical_not(has_below))
    def _():
        vel[0] = jnp.zeros((width_x, width_y), F32)
        for n in range(steps):
            fields[n, :, 0] = zero
        for k in range(steps - 1):
            weights[k, :, 0] = zero

    @pl.when(jnp.logical_not(has_above))
    def _():
        for n in range(steps):
            fields[n, :, depth + 1] = zero
        for k in range(steps - 1):
            weights[k, :, depth + 1] = zero

    rows = lax.broadcasted_iota(jnp.int32, (width_x, width_y), 0)
    cols = lax.broadcasted_iota(jnp.int32, (width_x, width_y), 1)

    def spread(ref, n, s, z):
        q = ref[n, s, z]
        along_x = next_x[z] * pltpu.roll(q, width_x - 1, 0) + prev_x[z] * pltpu.roll(q, 1, 0)
        along_y = next_y[z] * pltpu.roll(q, width_y - 1, 1) + prev_y[z] * pltpu.roll(q, 1, 1)
        along_z = vel[z] * ref[n, s, z + 1] + vel[z - 1] * ref[n, s, z - 1]
        return (along_x + along_y) + (along_z - centre[z] * q)

    def forward(n, which, z):
        for s in which:
            base = fields[0, s, z] if n == 0 else after[n - 1, s, z - 1]
            value = base + pres[z - 1] * spread(fields, n, s, z)
            before[n, s, z - 1] = value
            value = value * damp[z - 1]
            after[n, s, z - 1] = value
            if n + 1 < steps:
                fields[n + 1, s, z] = fields[n, s, z] + value

    def backward(n, which, z):
        k = steps - 1 - n
        part = None if k == 0 and 0 in which else grads[mine, z - 1]
        for s in which:
            value = adjoint[s, z - 1] + placed[n, s, z - 1]
            if k > 0:
                value = value + spread(weights, k - 1, s, z)
            term = before[n, s, z - 1] * value
            part = term if part is None else part + term
            if n > 0:
                scaled = value * damp[z - 1]
                adjoint[s, z - 1] = scaled
                weighted = pres[z - 1] * scaled
                if k > 0:
                    weighted = weighted + weights[k - 1, s, z]
                weights[k, s, z] = weighted
        grads[mine, z - 1] = part

    def over(low, high, step):
        size = max(g for g in (1, 2, 3) if (high - low) % g == 0)

        def run(i, carry):
            for j in range(size):
                step(low + i * size + j)
            return carry

        lax.fori_loop(0, (high - low) // size, run, 0)

    edges = (1, depth)
    middle = tuple(range(2, depth))

    for load in loads[:4]:
        load.wait()

    def coefficients(z):
        rho = density[z]
        v = 0.5 / rho
        vel[z] = v
        behind_x = jnp.where(rows == 0, 0.0, pltpu.roll(v, 1, 0))
        behind_y = jnp.where(cols == 0, 0.0, pltpu.roll(v, 1, 1))
        next_x[z] = jnp.where(rows == width_x - 1, 0.0, v)
        next_y[z] = jnp.where(cols == width_y - 1, 0.0, v)
        prev_x[z] = behind_x
        prev_y[z] = behind_y
        centre[z] = 3.0 * v + behind_x + behind_y
        c = pres[z - 1]
        pres[z - 1] = 0.5 * rho * c * c
        damp[z - 1] = 1.0 - damp[z - 1] * mask[z - 1].astype(F32)

    def add_below(z):
        centre[z] = centre[z] + vel[z - 1]

    over(1, depth + 1, coefficients)
    over(2, depth + 1, add_below)
    for load in loads[4:9]:
        load.wait()

    caps, channels = encoder.shape
    count = slots * caps
    lanes = -(-count // 128) * 128
    spare = lanes - count
    flat = [cells[pl.ds(r, 1), :] for r in range(slots)]
    if spare:
        flat.append(jnp.full((1, spare), -1, jnp.int32))
    flat = jnp.concatenate(flat, axis=1)
    plane_at = flat // width_y
    col_at = flat - plane_at * width_y
    pick_col = jnp.where(
        lax.broadcasted_iota(jnp.int32, (width_y, lanes), 0) == col_at, 1.0, 0.0
    ).astype(jnp.bfloat16)
    read_col = jnp.concatenate([pick_col, pick_col], axis=0)
    write_col = jnp.concatenate([pick_col, pick_col], axis=1)
    plane_twice = jnp.concatenate([plane_at, plane_at], axis=1)
    band = lax.broadcasted_iota(jnp.int32, (width_x, lanes), 0)
    band_twice = lax.broadcasted_iota(jnp.int32, (width_x, 2 * lanes), 0)

    pad = -(-slots * shots // 8) * 8
    slot_of = lax.broadcasted_iota(jnp.int32, (1, lanes), 1) // caps
    row_of = lax.broadcasted_iota(jnp.int32, (pad, lanes), 0)
    owns = [row_of == slot_of * shots + s for s in range(shots)]
    row_at = lax.broadcasted_iota(jnp.int32, (pad, channels), 0)
    live_row = jnp.zeros((pad, channels), F32)
    live_lane = jnp.zeros((1, lanes), F32)
    for r in range(slots):
        alive = live[r].astype(F32)
        live_row = jnp.where(row_at // shots == r, alive, live_row)
        live_lane = jnp.where(slot_of == r, alive, live_lane)
    filters = [encoder[...]] * slots
    if spare:
        filters.append(jnp.zeros((spare, channels), F32))
    filters = jnp.concatenate(filters, axis=0)

    def exact(a, b, contract):
        return lax.dot_general(
            a,
            b,
            (contract, ((), ())),
            precision=lax.Precision.HIGHEST,
            preferred_element_type=F32,
        )

    gram = exact(filters, filters, ((1,), (1,)))
    same = lax.broadcasted_iota(jnp.int32, (lanes, lanes), 0) // caps == slot_of
    gram_high, gram_low = split(jnp.where(same, gram, 0.0))
    gram = jnp.concatenate([gram_high, gram_high, gram_low], axis=0)

    goals = []
    for n in range(steps):
        signal = jnp.zeros((pad, channels), F32)
        for r in range(slots):
            for s in range(shots):
                signal = jnp.where(row_at == r * shots + s, target[r, s, pl.ds(n, 1), :], signal)
        wide = exact(signal * live_row, filters, ((1,), (1,)))
        goals.append(
            [
                jnp.sum(jnp.where(owns[s], wide, 0.0), axis=0, keepdims=True)
                for s in range(shots)
            ]
        )

    def sample(n, s, planes):
        values = jnp.concatenate([after[n, s, z - 1] for z in planes], axis=0)
        got = jnp.dot(
            jnp.concatenate(split(values), axis=1), read_col, preferred_element_type=F32
        )
        part = jnp.zeros((width_x, lanes), F32)
        for i, z in enumerate(planes):
            pick = band + (z - 1) * width_x == plane_at
            part = part + jnp.where(pick, got[i * width_x : (i + 1) * width_x], 0.0)
        return jnp.sum(part, axis=0, keepdims=True)

    def encode(n, found):
        table = jnp.zeros((pad, lanes), F32)
        for s in range(shots):
            table = jnp.where(owns[s], found[s], table)
        encoded = exact(table, filters, ((1,), (0,))) * live_row
        for r in range(slots):
            for s in range(shots):
                i = r * shots + s
                record[r, s, pl.ds(n, 1), :] = encoded[i : i + 1]

    def source(n, s, found):
        high, low = split(jnp.broadcast_to(found, (16, lanes)))
        wide = jnp.dot(
            jnp.concatenate([high, low, high], axis=1), gram, preferred_element_type=F32
        )
        return wide[0:1] * live_lane - goals[n][s]

    def place(n, s, value, planes):
        high, low = split(value)
        both = jnp.concatenate([high.astype(F32), low.astype(F32)], axis=1)
        spots = []
        for z in planes:
            pick = band_twice + (z - 1) * width_x == plane_twice
            spots.append(jnp.where(pick, both, 0.0).astype(jnp.bfloat16))
        put = lax.dot_general(
            jnp.concatenate(spots, axis=0),
            write_col,
            (((1,), (1,)), ((), ())),
            preferred_element_type=F32,
        )
        for i, z in enumerate(planes):
            placed[n, s, z - 1] = put[i * width_x : (i + 1) * width_x]

    last = steps - 1
    for n in range(steps):
        over(2, depth, functools.partial(forward, n, each))
        if n == last:
            found = [sample(n, s, middle) for s in each]
            loads[9].wait()
        if n == 0:

            @pl.when(has_below)
            def _():
                density_up.wait_recv()
                vel[0] = 0.5 / density[0]
                add_below(1)

        sources = []
        for s in each:
            arrive(rounds[n][s])
            for z in edges:
                forward(n, (s,), z)
            if n < last:
                start(rounds[n + 1][s])
            else:
                found[s] = found[s] + sample(n, s, edges)
                sources.append(source(n, s, found[s]))
                place(n, s, sources[s], edges)
                for z in edges:
                    backward(n, (s,), z)
                if n > 0:
                    start(rounds[steps][s])

    def share(k, low, size):
        planes = pl.ds(low, size)
        copies = []
        for j in range(1, group):
            copies.append(
                pltpu.make_async_remote_copy(
                    src_ref=grads.at[mine, planes],
                    dst_ref=grads.at[mine, planes],
                    send_sem=gsend_sem.at[k, j - 1],
                    recv_sem=grecv_sem.at[k, j - 1],
                    device_id={"shot": lax.rem(mine + j, group)},
                    device_id_type=MESH,
                )
            )
        return copies

    parts = [(1, depth - 2), (0, 1), (depth - 1, 1)]
    shares = [share(k, low, size) for k, (low, size) in enumerate(parts)]

    for s in each:
        place(last, s, sources[s], middle)
    over(2, depth, functools.partial(backward, last, each))
    for n in reversed(range(last)):
        k = last - n
        old = [sample(n, s, middle + edges) for s in each]
        for s in each:
            place(n, s, source(n, s, old[s]), middle + edges)
        over(2, depth, functools.partial(backward, n, each))
        if n == 0:
            for copy in shares[0]:
                copy.start()
        encode(n, old)
        if n == 0:
            encode(last, found)
        for s in each:
            arrive(rounds[steps + k - 1][s])
            for z in edges:
                backward(n, (s,), z)
            if n > 0:
                start(rounds[steps + k][s])
    if steps == 1:
        encode(last, found)
        for copy in shares[0]:
            copy.start()
    for copy in shares[1] + shares[2]:
        copy.start()

    for k, (low, size) in enumerate(parts):
        for copy in shares[k]:
            copy.wait_recv()
        planes = pl.ds(low, size)
        value = grads[0, planes]
        for t in range(1, group):
            value = value + grads[t, planes]
        total[planes] = -(mask[planes].astype(F32) * value)
    for pairs in rounds:
        for pair in pairs:
            sent(pair)

    @pl.when(has_above)
    def _():
        density_up.wait_send()

    for copies in shares:
        for copy in copies:
            copy.wait_send()


def deliver(record, total, record_hbm, total_hbm, sem):
    copies = [
        pltpu.make_async_copy(total, total_hbm, sem.at[0]),
        pltpu.make_async_copy(record, record_hbm, sem.at[1]),
    ]
    for copy in copies:
        copy.start()
    for copy in copies:
        copy.wait()


def solution(mesh):
    slabs, group = mesh.shape["slab"], mesh.shape["shot"]

    def body(
        pressure_init,
        adjoint_init,
        density,
        speed,
        admittance,
        bound_mask,
        rec_cells,
        rec_live,
        encoder,
        target,
    ):
        shots, depth, width_x, width_y = pressure_init.shape
        slots, caps = rec_cells.shape
        steps, channels = target.shape[2], target.shape[3]
        plane = (depth, width_x, width_y)
        padded = (shots, depth + 2, width_x, width_y)
        any_spec = pl.BlockSpec(memory_space=pl.ANY)
        vmem_spec = pl.BlockSpec(memory_space=pltpu.VMEM)

        def in_hbm(value):
            return pltpu.with_memory_space_constraint(value, pltpu.HBM)

        record, total = pl.pallas_call(
            functools.partial(kernel, slabs, group, steps, slots),
            out_shape=(
                pltpu.VMEM(target.shape, F32),
                pltpu.VMEM(plane, F32),
            ),
            in_specs=[any_spec] * 10,
            out_specs=(vmem_spec, vmem_spec),
            scratch_shapes=[
                pltpu.VMEM((steps,) + padded, F32),
                pltpu.VMEM((max(steps - 1, 1),) + padded, F32),
                pltpu.VMEM((depth + 1, width_x, width_y), F32),
                pltpu.VMEM((depth + 1, width_x, width_y), F32),
                pltpu.VMEM((depth + 1, width_x, width_y), F32),
                pltpu.VMEM((depth + 1, width_x, width_y), F32),
                pltpu.VMEM((depth + 1, width_x, width_y), F32),
                pltpu.VMEM((depth + 1, width_x, width_y), F32),
                pltpu.VMEM((depth + 1, width_x, width_y), F32),
                pltpu.VMEM(plane, F32),
                pltpu.VMEM(plane, F32),
                pltpu.VMEM(plane, jnp.int32),
                pltpu.VMEM((shots,) + plane, F32),
                pltpu.VMEM((steps, shots) + plane, F32),
                pltpu.VMEM((steps, shots) + plane, F32),
                pltpu.VMEM((steps, shots) + plane, F32),
                pltpu.VMEM((group,) + plane, F32),
                pltpu.VMEM((slots, caps), jnp.int32),
                pltpu.SMEM((slots,), jnp.int32),
                pltpu.VMEM((caps, channels), F32),
                pltpu.VMEM(target.shape, F32),
                pltpu.SemaphoreType.DMA((10,)),
                pltpu.SemaphoreType.DMA((2 * steps, shots, 3)),
                pltpu.SemaphoreType.DMA((2 * steps, shots, 3)),
                pltpu.SemaphoreType.DMA((3, max(group - 1, 1))),
                pltpu.SemaphoreType.DMA((3, max(group - 1, 1))),
            ],
            compiler_params=pltpu.CompilerParams(
                collective_id=0, has_side_effects=True, vmem_limit_bytes=48 * 1024 * 1024
            ),
        )(
            in_hbm(pressure_init),
            in_hbm(adjoint_init),
            in_hbm(density),
            in_hbm(speed),
            in_hbm(admittance),
            in_hbm(bound_mask),
            in_hbm(rec_cells),
            in_hbm(rec_live),
            in_hbm(encoder),
            in_hbm(target),
        )
        return pl.pallas_call(
            deliver,
            out_shape=(
                jax.ShapeDtypeStruct(target.shape, F32),
                jax.ShapeDtypeStruct(plane, F32),
            ),
            in_specs=[vmem_spec] * 2,
            out_specs=(any_spec, any_spec),
            scratch_shapes=[pltpu.SemaphoreType.DMA((2,))],
        )(
            pltpu.with_memory_space_constraint(record, pltpu.VMEM),
            pltpu.with_memory_space_constraint(total, pltpu.VMEM),
        )

    placed = (
        P("shot", "slab", None, None),
        P("shot", "slab", None, None),
        P("slab", None, None),
        P("slab", None, None),
        P("slab", None, None),
        P("slab", None, None),
        P("slab", None),
        P("slab"),
        P(),
        P("slab", "shot", None, None),
    )
    return jax.shard_map(
        body,
        mesh=mesh,
        in_specs=placed,
        out_specs=(P("slab", "shot", None, None), P("slab", None, None)),
        check_vma=False,
    )
```

```python
import functools

import jax
import jax.numpy as jnp
from jax import lax
from jax.experimental import pallas as pl
from jax.experimental.pallas import tpu as pltpu
from jax.sharding import PartitionSpec as P

MESH = pl.DeviceIdType.MESH
F32 = jnp.float32


def split(value):
    high = value.astype(jnp.bfloat16)
    return high, (value - high.astype(F32)).astype(jnp.bfloat16)


def kernel(
    slabs,
    group,
    steps,
    slots,
    pressure_hbm,
    adjoint_hbm,
    density_hbm,
    speed_hbm,
    admittance_hbm,
    mask_hbm,
    cells_hbm,
    live_hbm,
    encoder_hbm,
    target_hbm,
    record,
    total,
    fields,
    weights,
    density,
    vel,
    next_x,
    prev_x,
    next_y,
    prev_y,
    centre,
    pres,
    damp,
    mask,
    adjoint,
    before,
    after,
    placed,
    grads,
    cross_out,
    cross_in,
    cells,
    live,
    encoder,
    target,
    load_sem,
    send_sem,
    recv_sem,
    gsend_sem,
    grecv_sem,
    rho_sem,
    cross_sem,
):
    shots, depth, width_x, width_y = pressure_hbm.shape
    me = lax.axis_index("slab")
    mine = lax.axis_index("shot")
    has_below = me > 0
    has_above = me < slabs - 1

    inner = pl.ds(1, depth)
    pairs = [
        (density_hbm, density.at[inner]),
        (speed_hbm, pres),
        (admittance_hbm, damp),
        (mask_hbm, mask),
        (pressure_hbm, fields.at[0, :, inner]),
        (cells_hbm, cells),
        (live_hbm, live),
        (encoder_hbm, encoder),
        (target_hbm, target),
        (adjoint_hbm, adjoint),
    ]
    loads = [pltpu.make_async_copy(a, b, load_sem.at[i]) for i, (a, b) in enumerate(pairs)]
    for load in loads:
        load.start()

    barrier = pltpu.get_barrier_semaphore()

    @pl.when(has_below)
    def _():
        pl.semaphore_signal(barrier, inc=1, device_id={"slab": me - 1}, device_id_type=MESH)

    @pl.when(has_above)
    def _():
        pl.semaphore_signal(barrier, inc=1, device_id={"slab": me + 1}, device_id_type=MESH)

    for j in range(1, group):
        pl.semaphore_signal(
            barrier, inc=1, device_id={"shot": lax.rem(mine + j, group)}, device_id_type=MESH
        )

    def halo(k, s, source, into, first, last):
        down = pltpu.make_async_remote_copy(
            src_ref=source.at[s, pl.ds(first, 1)],
            dst_ref=into.at[s, pl.ds(depth + 1, 1)],
            send_sem=send_sem.at[k, s, 0],
            recv_sem=recv_sem.at[k, s, 0],
            device_id={"slab": me - 1},
            device_id_type=MESH,
        )
        up = pltpu.make_async_remote_copy(
            src_ref=source.at[s, pl.ds(last, 1)],
            dst_ref=into.at[s, pl.ds(0, 1)],
            send_sem=send_sem.at[k, s, 1],
            recv_sem=recv_sem.at[k, s, 1],
            device_id={"slab": me + 1},
            device_id_type=MESH,
        )
        return down, up

    def start(pair):
        down, up = pair

        @pl.when(has_below)
        def _():
            down.start()

        @pl.when(has_above)
        def _():
            up.start()

    def arrive(pair):
        down, up = pair

        @pl.when(has_above)
        def _():
            down.wait_recv()

        @pl.when(has_below)
        def _():
            up.wait_recv()

    def sent(pair):
        down, up = pair

        @pl.when(has_below)
        def _():
            down.wait_send()

        @pl.when(has_above)
        def _():
            up.wait_send()

    each = range(shots)
    rounds = [[halo(0, s, pressure_hbm, fields.at[0], 0, depth - 1) for s in each]]
    for n in range(1, steps):
        rounds.append([halo(n, s, fields.at[n], fields.at[n], 1, depth) for s in each])
    for k in range(steps - 2):
        rounds.append(
            [halo(steps + k, s, weights.at[k], weights.at[k], 1, depth) for s in each]
        )
    shared = group > 1 and width_x % (8 * group) == 0
    size_x = width_x // group if shared else width_x
    share_x = pl.ds(pl.multiple_of(mine * size_x, 8), size_x) if shared else pl.ds(0, size_x)
    density_up = pltpu.make_async_remote_copy(
        src_ref=density_hbm.at[depth - 1, share_x],
        dst_ref=density.at[0, share_x],
        send_sem=send_sem.at[0, 0, 2],
        recv_sem=recv_sem.at[0, 0, 2],
        device_id={"slab": me + 1},
        device_id_type=MESH,
    )
    density_swap = [
        pltpu.make_async_remote_copy(
            src_ref=density.at[0, share_x],
            dst_ref=density.at[0, share_x],
            send_sem=rho_sem.at[0, j - 1],
            recv_sem=rho_sem.at[1, j - 1],
            device_id={"shot": lax.rem(mine + j, group)},
            device_id_type=MESH,
        )
        for j in range(1, group if shared else 1)
    ]
    cross = tuple(
        pltpu.make_async_remote_copy(
            src_ref=cross_out.at[i],
            dst_ref=cross_in.at[i],
            send_sem=cross_sem.at[0, i],
            recv_sem=cross_sem.at[1, i],
            device_id={"slab": me + 2 * i - 1},
            device_id_type=MESH,
        )
        for i in range(2)
    )

    pl.semaphore_wait(
        barrier, has_below.astype(jnp.int32) + has_above.astype(jnp.int32) + (group - 1)
    )

    @pl.when(has_above)
    def _():
        density_up.start()

    for s in each:
        start(rounds[0][s])

    zero = jnp.zeros((shots, width_x, width_y), F32)

    @pl.when(jnp.logical_not(has_below))
    def _():
        vel[0] = jnp.zeros((width_x, width_y), F32)
        cross_in[1] = jnp.zeros((width_x, width_y), F32)
        for n in range(steps):
            fields[n, :, 0] = zero
        for k in range(steps - 2):
            weights[k, :, 0] = zero

    @pl.when(jnp.logical_not(has_above))
    def _():
        cross_in[0] = jnp.zeros((width_x, width_y), F32)
        for n in range(steps):
            fields[n, :, depth + 1] = zero
        for k in range(steps - 2):
            weights[k, :, depth + 1] = zero

    if steps > 1:
        weights[steps - 2, :, 0] = zero
        weights[steps - 2, :, depth + 1] = zero

    rows = lax.broadcasted_iota(jnp.int32, (width_x, width_y), 0)
    cols = lax.broadcasted_iota(jnp.int32, (width_x, width_y), 1)

    def spread(ref, n, s, z):
        q = ref[n, s, z]
        along_x = next_x[z] * pltpu.roll(q, width_x - 1, 0) + prev_x[z] * pltpu.roll(q, 1, 0)
        along_y = next_y[z] * pltpu.roll(q, width_y - 1, 1) + prev_y[z] * pltpu.roll(q, 1, 1)
        along_z = vel[z] * ref[n, s, z + 1] + vel[z - 1] * ref[n, s, z - 1]
        return (along_x + along_y) + (along_z - centre[z] * q)

    def forward(n, which, z):
        for s in which:
            base = fields[0, s, z] if n == 0 else after[n - 1, s, z - 1]
            value = base + pres[z - 1] * spread(fields, n, s, z)
            before[n, s, z - 1] = value
            value = value * damp[z - 1]
            after[n, s, z - 1] = value
            if n + 1 < steps:
                fields[n + 1, s, z] = fields[n, s, z] + value

    def backward(n, which, z):
        k = steps - 1 - n
        part = None if k == 0 and 0 in which else grads[mine, z - 1]
        for s in which:
            value = adjoint[s, z - 1] + placed[n, s, z - 1]
            if k > 0:
                value = value + spread(weights, k - 1, s, z)
            term = before[n, s, z - 1] * value
            part = term if part is None else part + term
            if n > 0:
                scaled = value * damp[z - 1]
                adjoint[s, z - 1] = scaled
                weighted = pres[z - 1] * scaled
                if k > 0:
                    weighted = weighted + weights[k - 1, s, z]
                weights[k, s, z] = weighted
        grads[mine, z - 1] = part

    def over(low, high, step):
        size = max(g for g in (1, 2, 3) if (high - low) % g == 0)

        def run(i, carry):
            for j in range(size):
                step(low + i * size + j)
            return carry

        lax.fori_loop(0, (high - low) // size, run, 0)

    edges = (1, depth)
    middle = tuple(range(2, depth))

    for load in loads[:4]:
        load.wait()

    def coefficients(z):
        rho = density[z]
        v = 0.5 / rho
        vel[z] = v
        behind_x = jnp.where(rows == 0, 0.0, pltpu.roll(v, 1, 0))
        behind_y = jnp.where(cols == 0, 0.0, pltpu.roll(v, 1, 1))
        next_x[z] = jnp.where(rows == width_x - 1, 0.0, v)
        next_y[z] = jnp.where(cols == width_y - 1, 0.0, v)
        prev_x[z] = behind_x
        prev_y[z] = behind_y
        centre[z] = 3.0 * v + behind_x + behind_y
        c = pres[z - 1]
        pres[z - 1] = 0.5 * rho * c * c
        damp[z - 1] = 1.0 - damp[z - 1] * mask[z - 1].astype(F32)

    def add_below(z):
        centre[z] = centre[z] + vel[z - 1]

    over(1, depth + 1, coefficients)
    over(2, depth + 1, add_below)
    for load in loads[4:9]:
        load.wait()

    caps, channels = encoder.shape
    count = slots * caps
    lanes = -(-count // 128) * 128
    spare = lanes - count
    flat = [cells[pl.ds(r, 1), :] for r in range(slots)]
    if spare:
        flat.append(jnp.full((1, spare), -1, jnp.int32))
    flat = jnp.concatenate(flat, axis=1)
    plane_at = flat // width_y
    col_at = flat - plane_at * width_y
    pick_col = jnp.where(
        lax.broadcasted_iota(jnp.int32, (width_y, lanes), 0) == col_at, 1.0, 0.0
    ).astype(jnp.bfloat16)
    read_col = jnp.concatenate([pick_col, pick_col], axis=0)
    write_col = jnp.concatenate([pick_col, pick_col], axis=1)
    plane_twice = jnp.concatenate([plane_at, plane_at], axis=1)
    band = lax.broadcasted_iota(jnp.int32, (width_x, lanes), 0)
    band_twice = lax.broadcasted_iota(jnp.int32, (width_x, 2 * lanes), 0)

    pad = -(-slots * shots // 8) * 8
    slot_of = lax.broadcasted_iota(jnp.int32, (1, lanes), 1) // caps
    row_of = lax.broadcasted_iota(jnp.int32, (pad, lanes), 0)
    owns = [row_of == slot_of * shots + s for s in range(shots)]
    row_at = lax.broadcasted_iota(jnp.int32, (pad, channels), 0)
    live_row = jnp.zeros((pad, channels), F32)
    live_lane = jnp.zeros((1, lanes), F32)
    for r in range(slots):
        alive = live[r].astype(F32)
        live_row = jnp.where(row_at // shots == r, alive, live_row)
        live_lane = jnp.where(slot_of == r, alive, live_lane)
    filters = [encoder[...]] * slots
    if spare:
        filters.append(jnp.zeros((spare, channels), F32))
    filters = jnp.concatenate(filters, axis=0)

    def exact(a, b, contract):
        return lax.dot_general(
            a,
            b,
            (contract, ((), ())),
            precision=lax.Precision.HIGHEST,
            preferred_element_type=F32,
        )

    gram = exact(filters, filters, ((1,), (1,)))
    same = lax.broadcasted_iota(jnp.int32, (lanes, lanes), 0) // caps == slot_of
    gram_high, gram_low = split(jnp.where(same, gram, 0.0))
    gram = jnp.concatenate([gram_high, gram_high, gram_low], axis=0)

    goals = []
    for n in range(steps):
        signal = jnp.zeros((pad, channels), F32)
        for r in range(slots):
            for s in range(shots):
                signal = jnp.where(row_at == r * shots + s, target[r, s, pl.ds(n, 1), :], signal)
        wide = exact(signal * live_row, filters, ((1,), (1,)))
        goals.append(
            [
                jnp.sum(jnp.where(owns[s], wide, 0.0), axis=0, keepdims=True)
                for s in range(shots)
            ]
        )

    def sample(n, planes):
        values = jnp.concatenate([after[n, s, z - 1] for s in each for z in planes], axis=0)
        got = jnp.dot(
            jnp.concatenate(split(values), axis=1), read_col, preferred_element_type=F32
        )
        found = []
        at = 0
        for s in each:
            part = jnp.zeros((width_x, lanes), F32)
            for z in planes:
                pick = band + (z - 1) * width_x == plane_at
                part = part + jnp.where(pick, got[at : at + width_x], 0.0)
                at += width_x
            found.append(jnp.sum(part, axis=0, keepdims=True))
        return found

    def encode(n, found):
        table = jnp.zeros((pad, lanes), F32)
        for s in range(shots):
            table = jnp.where(owns[s], found[s], table)
        encoded = exact(table, filters, ((1,), (0,))) * live_row
        for r in range(slots):
            for s in range(shots):
                i = r * shots + s
                record[r, s, pl.ds(n, 1), :] = encoded[i : i + 1]

    def source(n, found):
        rows_of = lax.broadcasted_iota(jnp.int32, (-(-shots // 16) * 16, lanes), 0)
        table = jnp.zeros(rows_of.shape, F32)
        for s in each:
            table = jnp.where(rows_of == s, found[s], table)
        high, low = split(table)
        wide = jnp.dot(
            jnp.concatenate([high, low, high], axis=1), gram, preferred_element_type=F32
        )
        return [wide[s : s + 1] * live_lane - goals[n][s] for s in each]

    def place(n, values, planes):
        spots = []
        for s in each:
            high, low = split(values[s])
            both = jnp.concatenate([high.astype(F32), low.astype(F32)], axis=1)
            for z in planes:
                pick = band_twice + (z - 1) * width_x == plane_twice
                spots.append(jnp.where(pick, both, 0.0).astype(jnp.bfloat16))
        put = lax.dot_general(
            jnp.concatenate(spots, axis=0),
            write_col,
            (((1,), (1,)), ((), ())),
            preferred_element_type=F32,
        )
        at = 0
        for s in each:
            for z in planes:
                placed[n, s, z - 1] = put[at : at + width_x]
                at += width_x

    @pl.when(has_below)
    def _():
        density_up.wait_recv()
        for copy in density_swap:
            copy.start()

    last = steps - 1
    for n in range(steps):
        over(2, depth, functools.partial(forward, n, each))
        if n == last:
            found = sample(n, middle)
            loads[9].wait()
        if n == 0:

            @pl.when(has_below)
            def _():
                for copy in density_swap:
                    copy.wait_recv()
                vel[0] = 0.5 / density[0]
                add_below(1)

        for s in each:
            arrive(rounds[n][s])
            for z in edges:
                forward(n, (s,), z)
            if n < last:
                start(rounds[n + 1][s])

    found = [a + b for a, b in zip(found, sample(last, edges))]
    sources = source(last, found)
    place(last, sources, edges)
    for z in edges:
        backward(last, each, z)

    def send_cross():
        for i, (z, beyond) in enumerate(((1, 0), (depth, depth + 1))):
            part = None
            for s in each:
                term = weights[steps - 2, s, z] * (fields[1, s, beyond] - fields[0, s, beyond])
                part = term if part is None else part + term
            cross_out[i] = part
        start(cross)

    if last > 1:
        for s in each:
            start(rounds[steps][s])
    elif last == 1:
        send_cross()

    def share(k, low, size):
        planes = pl.ds(low, size)
        copies = []
        for j in range(1, group):
            copies.append(
                pltpu.make_async_remote_copy(
                    src_ref=grads.at[mine, planes],
                    dst_ref=grads.at[mine, planes],
                    send_sem=gsend_sem.at[k, j - 1],
                    recv_sem=grecv_sem.at[k, j - 1],
                    device_id={"shot": lax.rem(mine + j, group)},
                    device_id_type=MESH,
                )
            )
        return copies

    parts = [(1, depth - 2), (0, 1), (depth - 1, 1)]
    shares = [share(k, low, size) for k, (low, size) in enumerate(parts)]

    place(last, sources, middle)
    over(2, depth, functools.partial(backward, last, each))
    for n in reversed(range(last)):
        k = last - n
        old = sample(n, middle + edges)
        place(n, source(n, old), middle + edges)
        if n == 0:
            over(1, depth + 1, functools.partial(backward, n, each))
            for copy in shares[0]:
                copy.start()
        else:
            over(2, depth, functools.partial(backward, n, each))
            for s in each:
                arrive(rounds[steps + k - 1][s])
            for z in edges:
                backward(n, each, z)
            if n > 1:
                for s in each:
                    start(rounds[steps + k][s])
            else:
                send_cross()
        encode(n, old)
    encode(last, found)
    if last > 0:
        arrive(cross)
        for i, (z, face) in enumerate(((depth, depth), (1, 0))):
            grads[mine, z - 1] = grads[mine, z - 1] + vel[face] / damp[z - 1] * cross_in[i]
    else:
        for copy in shares[0]:
            copy.start()
    for copy in shares[1] + shares[2]:
        copy.start()

    for k, (low, size) in enumerate(parts):
        for copy in shares[k]:
            copy.wait_recv()
        planes = pl.ds(low, size)
        value = grads[0, planes]
        for t in range(1, group):
            value = value + grads[t, planes]
        total[planes] = -(mask[planes].astype(F32) * value)
    for pairs in rounds:
        for pair in pairs:
            sent(pair)

    if last > 0:
        sent(cross)

    @pl.when(has_above)
    def _():
        density_up.wait_send()

    @pl.when(has_below)
    def _():
        for copy in density_swap:
            copy.wait_send()

    for copies in shares:
        for copy in copies:
            copy.wait_send()


def deliver(record, total, record_hbm, total_hbm, sem):
    copies = [
        pltpu.make_async_copy(total, total_hbm, sem.at[0]),
        pltpu.make_async_copy(record, record_hbm, sem.at[1]),
    ]
    for copy in copies:
        copy.start()
    for copy in copies:
        copy.wait()


def solution(mesh):
    slabs, group = mesh.shape["slab"], mesh.shape["shot"]

    def body(
        pressure_init,
        adjoint_init,
        density,
        speed,
        admittance,
        bound_mask,
        rec_cells,
        rec_live,
        encoder,
        target,
    ):
        shots, depth, width_x, width_y = pressure_init.shape
        slots, caps = rec_cells.shape
        steps, channels = target.shape[2], target.shape[3]
        plane = (depth, width_x, width_y)
        padded = (shots, depth + 2, width_x, width_y)
        any_spec = pl.BlockSpec(memory_space=pl.ANY)
        vmem_spec = pl.BlockSpec(memory_space=pltpu.VMEM)

        def in_hbm(value):
            return pltpu.with_memory_space_constraint(value, pltpu.HBM)

        record, total = pl.pallas_call(
            functools.partial(kernel, slabs, group, steps, slots),
            out_shape=(
                pltpu.VMEM(target.shape, F32),
                pltpu.VMEM(plane, F32),
            ),
            in_specs=[any_spec] * 10,
            out_specs=(vmem_spec, vmem_spec),
            scratch_shapes=[
                pltpu.VMEM((steps,) + padded, F32),
                pltpu.VMEM((max(steps - 1, 1),) + padded, F32),
                pltpu.VMEM((depth + 1, width_x, width_y), F32),
                pltpu.VMEM((depth + 1, width_x, width_y), F32),
                pltpu.VMEM((depth + 1, width_x, width_y), F32),
                pltpu.VMEM((depth + 1, width_x, width_y), F32),
                pltpu.VMEM((depth + 1, width_x, width_y), F32),
                pltpu.VMEM((depth + 1, width_x, width_y), F32),
                pltpu.VMEM((depth + 1, width_x, width_y), F32),
                pltpu.VMEM(plane, F32),
                pltpu.VMEM(plane, F32),
                pltpu.VMEM(plane, jnp.int32),
                pltpu.VMEM((shots,) + plane, F32),
                pltpu.VMEM((steps, shots) + plane, F32),
                pltpu.VMEM((steps, shots) + plane, F32),
                pltpu.VMEM((steps, shots) + plane, F32),
                pltpu.VMEM((group,) + plane, F32),
                pltpu.VMEM((2, width_x, width_y), F32),
                pltpu.VMEM((2, width_x, width_y), F32),
                pltpu.VMEM((slots, caps), jnp.int32),
                pltpu.SMEM((slots,), jnp.int32),
                pltpu.VMEM((caps, channels), F32),
                pltpu.VMEM(target.shape, F32),
                pltpu.SemaphoreType.DMA((10,)),
                pltpu.SemaphoreType.DMA((2 * steps, shots, 3)),
                pltpu.SemaphoreType.DMA((2 * steps, shots, 3)),
                pltpu.SemaphoreType.DMA((3, max(group - 1, 1))),
                pltpu.SemaphoreType.DMA((3, max(group - 1, 1))),
                pltpu.SemaphoreType.DMA((2, max(group - 1, 1))),
                pltpu.SemaphoreType.DMA((2, 2)),
            ],
            compiler_params=pltpu.CompilerParams(
                collective_id=0, has_side_effects=True, vmem_limit_bytes=48 * 1024 * 1024
            ),
        )(
            in_hbm(pressure_init),
            in_hbm(adjoint_init),
            in_hbm(density),
            in_hbm(speed),
            in_hbm(admittance),
            in_hbm(bound_mask),
            in_hbm(rec_cells),
            in_hbm(rec_live),
            in_hbm(encoder),
            in_hbm(target),
        )
        return pl.pallas_call(
            deliver,
            out_shape=(
                jax.ShapeDtypeStruct(target.shape, F32),
                jax.ShapeDtypeStruct(plane, F32),
            ),
            in_specs=[vmem_spec] * 2,
            out_specs=(any_spec, any_spec),
            scratch_shapes=[pltpu.SemaphoreType.DMA((2,))],
        )(
            pltpu.with_memory_space_constraint(record, pltpu.VMEM),
            pltpu.with_memory_space_constraint(total, pltpu.VMEM),
        )

    placed = (
        P("shot", "slab", None, None),
        P("shot", "slab", None, None),
        P("slab", None, None),
        P("slab", None, None),
        P("slab", None, None),
        P("slab", None, None),
        P("slab", None),
        P("slab"),
        P(),
        P("slab", "shot", None, None),
    )
    return jax.shard_map(
        body,
        mesh=mesh,
        in_specs=placed,
        out_specs=(P("slab", "shot", None, None), P("slab", None, None)),
        check_vma=False,
    )
```

```python
import functools

import jax
import jax.numpy as jnp
from jax import lax
from jax.experimental import pallas as pl
from jax.experimental.pallas import tpu as pltpu
from jax.sharding import PartitionSpec as P

MESH = pl.DeviceIdType.MESH
F32 = jnp.float32


def split(value):
    high = value.astype(jnp.bfloat16)
    return high, (value - high.astype(F32)).astype(jnp.bfloat16)


def kernel(
    slabs,
    group,
    steps,
    slots,
    pressure_hbm,
    adjoint_hbm,
    density_hbm,
    speed_hbm,
    admittance_hbm,
    mask_hbm,
    cells_hbm,
    live_hbm,
    encoder_hbm,
    target_hbm,
    record,
    total,
    fields,
    weights,
    density,
    vel,
    next_x,
    prev_x,
    next_y,
    prev_y,
    centre,
    pres,
    damp,
    mask,
    adjoint,
    before,
    after,
    placed,
    grads,
    cross_out,
    cross_in,
    early,
    coef_out,
    coef_in,
    cells,
    live,
    encoder,
    target,
    load_sem,
    send_sem,
    recv_sem,
    gsend_sem,
    grecv_sem,
    swap_sem,
    coef_sem,
    cross_sem,
):
    shots, depth, width_x, width_y = pressure_hbm.shape
    me = lax.axis_index("slab")
    mine = lax.axis_index("shot")
    has_below = me > 0
    has_above = me < slabs - 1

    barrier = pltpu.get_barrier_semaphore()

    @pl.when(has_below)
    def _():
        pl.semaphore_signal(barrier, inc=1, device_id={"slab": me - 1}, device_id_type=MESH)

    @pl.when(has_above)
    def _():
        pl.semaphore_signal(barrier, inc=1, device_id={"slab": me + 1}, device_id_type=MESH)

    for j in range(1, group):
        pl.semaphore_signal(
            barrier, inc=1, device_id={"shot": lax.rem(mine + j, group)}, device_id_type=MESH
        )

    inner = pl.ds(1, depth)
    pairs = [
        (pressure_hbm, fields.at[0, :, inner]),
        (density_hbm, density.at[inner]),
        (speed_hbm, pres),
        (admittance_hbm, damp),
        (mask_hbm, mask),
        (cells_hbm, cells),
        (live_hbm, live),
        (encoder_hbm, encoder),
        (target_hbm, target),
        (adjoint_hbm, adjoint),
    ]
    loads = [pltpu.make_async_copy(a, b, load_sem.at[i]) for i, (a, b) in enumerate(pairs)]
    for load in loads:
        load.start()

    def halo(k, s, source, into, first, last):
        down = pltpu.make_async_remote_copy(
            src_ref=source.at[s, pl.ds(first, 1)],
            dst_ref=into.at[s, pl.ds(depth + 1, 1)],
            send_sem=send_sem.at[k, s, 0],
            recv_sem=recv_sem.at[k, s, 0],
            device_id={"slab": me - 1},
            device_id_type=MESH,
        )
        up = pltpu.make_async_remote_copy(
            src_ref=source.at[s, pl.ds(last, 1)],
            dst_ref=into.at[s, pl.ds(0, 1)],
            send_sem=send_sem.at[k, s, 1],
            recv_sem=recv_sem.at[k, s, 1],
            device_id={"slab": me + 1},
            device_id_type=MESH,
        )
        return down, up

    def start(pair):
        down, up = pair

        @pl.when(has_below)
        def _():
            down.start()

        @pl.when(has_above)
        def _():
            up.start()

    def arrive(pair):
        down, up = pair

        @pl.when(has_above)
        def _():
            down.wait_recv()

        @pl.when(has_below)
        def _():
            up.wait_recv()

    def sent(pair):
        down, up = pair

        @pl.when(has_below)
        def _():
            down.wait_send()

        @pl.when(has_above)
        def _():
            up.wait_send()

    each = range(shots)
    rounds = [[halo(0, s, fields.at[0], fields.at[0], 1, depth) for s in each]]
    if steps > 1:
        rounds.append([halo(1, s, early, fields.at[1], 0, 1) for s in each])
    for n in range(2, steps):
        rounds.append([halo(n, s, fields.at[n], fields.at[n], 1, depth) for s in each])
    for k in range(steps - 2):
        rounds.append(
            [halo(steps + k, s, weights.at[k], weights.at[k], 1, depth) for s in each]
        )
    shared = group > 1 and width_x % (8 * group) == 0
    size_x = width_x // group if shared else width_x
    share_x = pl.ds(pl.multiple_of(mine * size_x, 8), size_x) if shared else pl.ds(0, size_x)
    coef_parts = (pl.ds(0, 1), pl.ds(1, 2))
    coefs = tuple(
        pltpu.make_async_remote_copy(
            src_ref=coef_out.at[coef_parts[i], share_x],
            dst_ref=coef_in.at[coef_parts[i], share_x],
            send_sem=coef_sem.at[0, i],
            recv_sem=coef_sem.at[1, i],
            device_id={"slab": me + 2 * i - 1},
            device_id_type=MESH,
        )
        for i in range(2)
    )
    swaps = [
        tuple(
            pltpu.make_async_remote_copy(
                src_ref=coef_in.at[coef_parts[i], share_x],
                dst_ref=coef_in.at[coef_parts[i], share_x],
                send_sem=swap_sem.at[0, i, j - 1],
                recv_sem=swap_sem.at[1, i, j - 1],
                device_id={"shot": lax.rem(mine + j, group)},
                device_id_type=MESH,
            )
            for i in range(2)
        )
        for j in range(1, group if shared else 1)
    ]
    cross = tuple(
        pltpu.make_async_remote_copy(
            src_ref=cross_out.at[i],
            dst_ref=cross_in.at[i],
            send_sem=cross_sem.at[0, i],
            recv_sem=cross_sem.at[1, i],
            device_id={"slab": me + 2 * i - 1},
            device_id_type=MESH,
        )
        for i in range(2)
    )

    zero = jnp.zeros((shots, width_x, width_y), F32)

    @pl.when(jnp.logical_not(has_below))
    def _():
        vel[0] = jnp.zeros((width_x, width_y), F32)
        cross_in[1] = jnp.zeros((width_x, width_y), F32)
        for n in range(steps):
            fields[n, :, 0] = zero
        for k in range(steps - 2):
            weights[k, :, 0] = zero

    @pl.when(jnp.logical_not(has_above))
    def _():
        cross_in[0] = jnp.zeros((width_x, width_y), F32)
        for n in range(steps):
            fields[n, :, depth + 1] = zero
        for k in range(steps - 2):
            weights[k, :, depth + 1] = zero

    if steps > 1:
        weights[steps - 2, :, 0] = zero
        weights[steps - 2, :, depth + 1] = zero

    rows = lax.broadcasted_iota(jnp.int32, (width_x, width_y), 0)
    cols = lax.broadcasted_iota(jnp.int32, (width_x, width_y), 1)

    def level(q, z):
        along_x = next_x[z] * pltpu.roll(q, width_x - 1, 0) + prev_x[z] * pltpu.roll(q, 1, 0)
        along_y = next_y[z] * pltpu.roll(q, width_y - 1, 1) + prev_y[z] * pltpu.roll(q, 1, 1)
        return along_x + along_y

    def spread(ref, n, s, z):
        q = ref[n, s, z]
        along_z = vel[z] * ref[n, s, z + 1] + vel[z - 1] * ref[n, s, z - 1]
        return level(q, z) + (along_z - centre[z] * q)

    def forward(n, which, z):
        for s in which:
            base = fields[0, s, z] if n == 0 else after[n - 1, s, z - 1]
            value = base + pres[z - 1] * spread(fields, n, s, z)
            before[n, s, z - 1] = value
            value = value * damp[z - 1]
            after[n, s, z - 1] = value
            if n + 1 < steps:
                fields[n + 1, s, z] = fields[n, s, z] + value

    def backward(n, which, z):
        k = steps - 1 - n
        part = None if k == 0 and 0 in which else grads[mine, z - 1]
        for s in which:
            value = adjoint[s, z - 1] + placed[n, s, z - 1]
            if k > 0:
                value = value + spread(weights, k - 1, s, z)
            term = before[n, s, z - 1] * value
            part = term if part is None else part + term
            if n > 0:
                scaled = value * damp[z - 1]
                adjoint[s, z - 1] = scaled
                weighted = pres[z - 1] * scaled
                if k > 0:
                    weighted = weighted + weights[k - 1, s, z]
                weights[k, s, z] = weighted
        grads[mine, z - 1] = part

    def over(low, high, step):
        size = max(g for g in (1, 2, 3) if (high - low) % g == 0)

        def run(i, carry):
            for j in range(size):
                step(low + i * size + j)
            return carry

        lax.fori_loop(0, (high - low) // size, run, 0)

    edges = (1, depth)
    middle = tuple(range(2, depth))

    for load in loads[:5]:
        load.wait()

    def coefficients(z):
        rho = density[z]
        v = 0.5 / rho
        vel[z] = v
        behind_x = jnp.where(rows == 0, 0.0, pltpu.roll(v, 1, 0))
        behind_y = jnp.where(cols == 0, 0.0, pltpu.roll(v, 1, 1))
        next_x[z] = jnp.where(rows == width_x - 1, 0.0, v)
        next_y[z] = jnp.where(cols == width_y - 1, 0.0, v)
        prev_x[z] = behind_x
        prev_y[z] = behind_y
        centre[z] = 3.0 * v + behind_x + behind_y
        c = pres[z - 1]
        pres[z - 1] = 0.5 * rho * c * c
        damp[z - 1] = 1.0 - damp[z - 1] * mask[z - 1].astype(F32)

    def add_below(z):
        centre[z] = centre[z] + vel[z - 1]

    over(1, depth + 1, coefficients)
    over(2, depth + 1, add_below)
    for i, z in enumerate(edges):
        coef_out[i] = damp[z - 1] * pres[z - 1]
    coef_out[2] = vel[depth]

    pl.semaphore_wait(
        barrier, has_below.astype(jnp.int32) + has_above.astype(jnp.int32) + (group - 1)
    )
    start(coefs)
    for s in each:
        start(rounds[0][s])
    if steps > 1:
        for s in each:
            for i, (z, beside) in enumerate(((1, 2), (depth, depth - 1))):
                q = fields[0, s, z]
                near = level(q, z) + vel[min(z, beside)] * fields[0, s, beside] - centre[z] * q
                early[s, i] = q + (q + pres[z - 1] * near) * damp[z - 1]
            start(rounds[1][s])

    for load in loads[5:9]:
        load.wait()

    caps, channels = encoder.shape
    count = slots * caps
    lanes = -(-count // 128) * 128
    spare = lanes - count
    flat = [cells[pl.ds(r, 1), :] for r in range(slots)]
    if spare:
        flat.append(jnp.full((1, spare), -1, jnp.int32))
    flat = jnp.concatenate(flat, axis=1)
    plane_at = flat // width_y
    col_at = flat - plane_at * width_y
    pick_col = jnp.where(
        lax.broadcasted_iota(jnp.int32, (width_y, lanes), 0) == col_at, 1.0, 0.0
    ).astype(jnp.bfloat16)
    read_col = jnp.concatenate([pick_col, pick_col], axis=0)
    write_col = jnp.concatenate([pick_col, pick_col], axis=1)
    plane_twice = jnp.concatenate([plane_at, plane_at], axis=1)
    band = lax.broadcasted_iota(jnp.int32, (width_x, lanes), 0)
    band_twice = lax.broadcasted_iota(jnp.int32, (width_x, 2 * lanes), 0)

    pad = -(-slots * shots // 8) * 8
    slot_of = lax.broadcasted_iota(jnp.int32, (1, lanes), 1) // caps
    row_of = lax.broadcasted_iota(jnp.int32, (pad, lanes), 0)
    owns = [row_of == slot_of * shots + s for s in range(shots)]
    row_at = lax.broadcasted_iota(jnp.int32, (pad, channels), 0)
    live_row = jnp.zeros((pad, channels), F32)
    live_lane = jnp.zeros((1, lanes), F32)
    for r in range(slots):
        alive = live[r].astype(F32)
        live_row = jnp.where(row_at // shots == r, alive, live_row)
        live_lane = jnp.where(slot_of == r, alive, live_lane)
    filters = [encoder[...]] * slots
    if spare:
        filters.append(jnp.zeros((spare, channels), F32))
    filters = jnp.concatenate(filters, axis=0)

    def exact(a, b, contract):
        return lax.dot_general(
            a,
            b,
            (contract, ((), ())),
            precision=lax.Precision.HIGHEST,
            preferred_element_type=F32,
        )

    gram = exact(filters, filters, ((1,), (1,)))
    same = lax.broadcasted_iota(jnp.int32, (lanes, lanes), 0) // caps == slot_of
    gram_high, gram_low = split(jnp.where(same, gram, 0.0))
    gram = jnp.concatenate([gram_high, gram_high, gram_low], axis=0)

    goals = []
    for n in range(steps):
        signal = jnp.zeros((pad, channels), F32)
        for r in range(slots):
            for s in range(shots):
                signal = jnp.where(row_at == r * shots + s, target[r, s, pl.ds(n, 1), :], signal)
        wide = exact(signal * live_row, filters, ((1,), (1,)))
        goals.append(
            [
                jnp.sum(jnp.where(owns[s], wide, 0.0), axis=0, keepdims=True)
                for s in range(shots)
            ]
        )

    def sample(n, planes):
        values = jnp.concatenate([after[n, s, z - 1] for s in each for z in planes], axis=0)
        got = jnp.dot(
            jnp.concatenate(split(values), axis=1), read_col, preferred_element_type=F32
        )
        found = []
        at = 0
        for s in each:
            part = jnp.zeros((width_x, lanes), F32)
            for z in planes:
                pick = band + (z - 1) * width_x == plane_at
                part = part + jnp.where(pick, got[at : at + width_x], 0.0)
                at += width_x
            found.append(jnp.sum(part, axis=0, keepdims=True))
        return found

    def encode(n, found):
        table = jnp.zeros((pad, lanes), F32)
        for s in range(shots):
            table = jnp.where(owns[s], found[s], table)
        encoded = exact(table, filters, ((1,), (0,))) * live_row
        for r in range(slots):
            for s in range(shots):
                i = r * shots + s
                record[r, s, pl.ds(n, 1), :] = encoded[i : i + 1]

    def source(n, found):
        rows_of = lax.broadcasted_iota(jnp.int32, (-(-shots // 16) * 16, lanes), 0)
        table = jnp.zeros(rows_of.shape, F32)
        for s in each:
            table = jnp.where(rows_of == s, found[s], table)
        high, low = split(table)
        wide = jnp.dot(
            jnp.concatenate([high, low, high], axis=1), gram, preferred_element_type=F32
        )
        return [wide[s : s + 1] * live_lane - goals[n][s] for s in each]

    def place(n, values, planes):
        spots = []
        for s in each:
            high, low = split(values[s])
            both = jnp.concatenate([high.astype(F32), low.astype(F32)], axis=1)
            for z in planes:
                pick = band_twice + (z - 1) * width_x == plane_twice
                spots.append(jnp.where(pick, both, 0.0).astype(jnp.bfloat16))
        put = lax.dot_general(
            jnp.concatenate(spots, axis=0),
            write_col,
            (((1,), (1,)), ((), ())),
            preferred_element_type=F32,
        )
        at = 0
        for s in each:
            for z in planes:
                placed[n, s, z - 1] = put[at : at + width_x]
                at += width_x

    last = steps - 1
    for n in range(steps):
        over(2, depth, functools.partial(forward, n, each))
        if n == last:
            found = sample(n, middle)
            loads[9].wait()
        if n == 0:
            arrive(coefs)

            @pl.when(has_above)
            def _():
                for pair in swaps:
                    pair[0].start()

            @pl.when(has_below)
            def _():
                for pair in swaps:
                    pair[1].start()

            for pair in swaps:
                arrive(pair)

            @pl.when(has_below)
            def _():
                vel[0] = coef_in[2]
                add_below(1)

        for s in each:
            arrive(rounds[n][s])
        if n == 1:

            @pl.when(has_above)
            def _():
                rate = coef_in[0] * vel[depth]
                for s in each:
                    fields[1, s, depth + 1] = fields[1, s, depth + 1] + rate * (
                        fields[0, s, depth] - fields[0, s, depth + 1]
                    )

            @pl.when(has_below)
            def _():
                rate = coef_in[1] * vel[0]
                for s in each:
                    fields[1, s, 0] = fields[1, s, 0] + rate * fields[0, s, 1]

        for z in edges:
            forward(n, each, z)
        if 0 < n < last:
            for s in each:
                start(rounds[n + 1][s])

    found = [a + b for a, b in zip(found, sample(last, edges))]
    sources = source(last, found)
    place(last, sources, edges)
    for z in edges:
        backward(last, each, z)

    def send_cross():
        for i, (z, beyond) in enumerate(((1, 0), (depth, depth + 1))):
            part = None
            for s in each:
                term = weights[steps - 2, s, z] * (fields[1, s, beyond] - fields[0, s, beyond])
                part = term if part is None else part + term
            cross_out[i] = part
        start(cross)

    if last > 1:
        for s in each:
            start(rounds[steps][s])
    elif last == 1:
        send_cross()

    def share(k, low, size):
        planes = pl.ds(low, size)
        copies = []
        for j in range(1, group):
            copies.append(
                pltpu.make_async_remote_copy(
                    src_ref=grads.at[mine, planes],
                    dst_ref=grads.at[mine, planes],
                    send_sem=gsend_sem.at[k, j - 1],
                    recv_sem=grecv_sem.at[k, j - 1],
                    device_id={"shot": lax.rem(mine + j, group)},
                    device_id_type=MESH,
                )
            )
        return copies

    parts = [(1, depth - 2), (0, 1), (depth - 1, 1)]
    shares = [share(k, low, size) for k, (low, size) in enumerate(parts)]

    place(last, sources, middle)
    over(2, depth, functools.partial(backward, last, each))
    for n in reversed(range(last)):
        k = last - n
        old = sample(n, middle + edges)
        place(n, source(n, old), middle + edges)
        if n == 0:
            over(1, depth + 1, functools.partial(backward, n, each))
            for copy in shares[0]:
                copy.start()
        else:
            over(2, depth, functools.partial(backward, n, each))
            for s in each:
                arrive(rounds[steps + k - 1][s])
            for z in edges:
                backward(n, each, z)
            if n > 1:
                for s in each:
                    start(rounds[steps + k][s])
            else:
                send_cross()
        encode(n, old)
    encode(last, found)
    if last > 0:
        ratios = [vel[face] / damp[z - 1] for z, face in ((depth, depth), (1, 0))]
        arrive(cross)
        for i, z in enumerate((depth, 1)):
            grads[mine, z - 1] = grads[mine, z - 1] + ratios[i] * cross_in[i]
    else:
        for copy in shares[0]:
            copy.start()
    for copy in shares[1] + shares[2]:
        copy.start()

    for k, (low, size) in enumerate(parts):
        for copy in shares[k]:
            copy.wait_recv()
        planes = pl.ds(low, size)
        value = grads[0, planes]
        for t in range(1, group):
            value = value + grads[t, planes]
        total[planes] = -(mask[planes].astype(F32) * value)
    for pairs in rounds:
        for pair in pairs:
            sent(pair)

    if last > 0:
        sent(cross)
    sent(coefs)

    @pl.when(has_above)
    def _():
        for pair in swaps:
            pair[0].wait_send()

    @pl.when(has_below)
    def _():
        for pair in swaps:
            pair[1].wait_send()

    for copies in shares:
        for copy in copies:
            copy.wait_send()


def deliver(record, total, record_hbm, total_hbm, sem):
    copies = [
        pltpu.make_async_copy(total, total_hbm, sem.at[0]),
        pltpu.make_async_copy(record, record_hbm, sem.at[1]),
    ]
    for copy in copies:
        copy.start()
    for copy in copies:
        copy.wait()


def solution(mesh):
    slabs, group = mesh.shape["slab"], mesh.shape["shot"]

    def body(
        pressure_init,
        adjoint_init,
        density,
        speed,
        admittance,
        bound_mask,
        rec_cells,
        rec_live,
        encoder,
        target,
    ):
        shots, depth, width_x, width_y = pressure_init.shape
        slots, caps = rec_cells.shape
        steps, channels = target.shape[2], target.shape[3]
        plane = (depth, width_x, width_y)
        padded = (shots, depth + 2, width_x, width_y)
        any_spec = pl.BlockSpec(memory_space=pl.ANY)
        vmem_spec = pl.BlockSpec(memory_space=pltpu.VMEM)

        def in_hbm(value):
            return pltpu.with_memory_space_constraint(value, pltpu.HBM)

        record, total = pl.pallas_call(
            functools.partial(kernel, slabs, group, steps, slots),
            out_shape=(
                pltpu.VMEM(target.shape, F32),
                pltpu.VMEM(plane, F32),
            ),
            in_specs=[any_spec] * 10,
            out_specs=(vmem_spec, vmem_spec),
            scratch_shapes=[
                pltpu.VMEM((steps,) + padded, F32),
                pltpu.VMEM((max(steps - 1, 1),) + padded, F32),
                pltpu.VMEM((depth + 1, width_x, width_y), F32),
                pltpu.VMEM((depth + 1, width_x, width_y), F32),
                pltpu.VMEM((depth + 1, width_x, width_y), F32),
                pltpu.VMEM((depth + 1, width_x, width_y), F32),
                pltpu.VMEM((depth + 1, width_x, width_y), F32),
                pltpu.VMEM((depth + 1, width_x, width_y), F32),
                pltpu.VMEM((depth + 1, width_x, width_y), F32),
                pltpu.VMEM(plane, F32),
                pltpu.VMEM(plane, F32),
                pltpu.VMEM(plane, jnp.int32),
                pltpu.VMEM((shots,) + plane, F32),
                pltpu.VMEM((steps, shots) + plane, F32),
                pltpu.VMEM((steps, shots) + plane, F32),
                pltpu.VMEM((steps, shots) + plane, F32),
                pltpu.VMEM((group,) + plane, F32),
                pltpu.VMEM((2, width_x, width_y), F32),
                pltpu.VMEM((2, width_x, width_y), F32),
                pltpu.VMEM((shots, 2, width_x, width_y), F32),
                pltpu.VMEM((3, width_x, width_y), F32),
                pltpu.VMEM((3, width_x, width_y), F32),
                pltpu.VMEM((slots, caps), jnp.int32),
                pltpu.SMEM((slots,), jnp.int32),
                pltpu.VMEM((caps, channels), F32),
                pltpu.VMEM(target.shape, F32),
                pltpu.SemaphoreType.DMA((10,)),
                pltpu.SemaphoreType.DMA((2 * steps, shots, 3)),
                pltpu.SemaphoreType.DMA((2 * steps, shots, 3)),
                pltpu.SemaphoreType.DMA((3, max(group - 1, 1))),
                pltpu.SemaphoreType.DMA((3, max(group - 1, 1))),
                pltpu.SemaphoreType.DMA((2, 2, max(group - 1, 1))),
                pltpu.SemaphoreType.DMA((2, 2)),
                pltpu.SemaphoreType.DMA((2, 2)),
            ],
            compiler_params=pltpu.CompilerParams(
                collective_id=0, has_side_effects=True, vmem_limit_bytes=48 * 1024 * 1024
            ),
        )(
            in_hbm(pressure_init),
            in_hbm(adjoint_init),
            in_hbm(density),
            in_hbm(speed),
            in_hbm(admittance),
            in_hbm(bound_mask),
            in_hbm(rec_cells),
            in_hbm(rec_live),
            in_hbm(encoder),
            in_hbm(target),
        )
        return pl.pallas_call(
            deliver,
            out_shape=(
                jax.ShapeDtypeStruct(target.shape, F32),
                jax.ShapeDtypeStruct(plane, F32),
            ),
            in_specs=[vmem_spec] * 2,
            out_specs=(any_spec, any_spec),
            scratch_shapes=[pltpu.SemaphoreType.DMA((2,))],
        )(
            pltpu.with_memory_space_constraint(record, pltpu.VMEM),
            pltpu.with_memory_space_constraint(total, pltpu.VMEM),
        )

    placed = (
        P("shot", "slab", None, None),
        P("shot", "slab", None, None),
        P("slab", None, None),
        P("slab", None, None),
        P("slab", None, None),
        P("slab", None, None),
        P("slab", None),
        P("slab"),
        P(),
        P("slab", "shot", None, None),
    )
    return jax.shard_map(
        body,
        mesh=mesh,
        in_specs=placed,
        out_specs=(P("slab", "shot", None, None), P("slab", None, None)),
        check_vma=False,
    )
```

```python
import functools

import jax
import jax.numpy as jnp
from jax import lax
from jax.experimental import pallas as pl
from jax.experimental.pallas import tpu as pltpu
from jax.sharding import PartitionSpec as P

MESH = pl.DeviceIdType.MESH
F32 = jnp.float32


def split(value):
    high = value.astype(jnp.bfloat16)
    return high, (value - high.astype(F32)).astype(jnp.bfloat16)


def kernel(
    slabs,
    group,
    steps,
    slots,
    pressure_hbm,
    adjoint_hbm,
    density_hbm,
    speed_hbm,
    admittance_hbm,
    mask_hbm,
    cells_hbm,
    live_hbm,
    encoder_hbm,
    target_hbm,
    record,
    total,
    fields,
    weights,
    density,
    vel,
    next_x,
    prev_x,
    next_y,
    prev_y,
    centre,
    pres,
    damp,
    mask,
    adjoint,
    before,
    after,
    placed,
    grads,
    cross_out,
    cross_in,
    early,
    coef_out,
    coef_in,
    cells,
    live,
    encoder,
    target,
    load_sem,
    send_sem,
    recv_sem,
    gsend_sem,
    grecv_sem,
    swap_sem,
    coef_sem,
    cross_sem,
):
    shots, depth, width_x, width_y = pressure_hbm.shape
    me = lax.axis_index("slab")
    mine = lax.axis_index("shot")
    has_below = me > 0
    has_above = me < slabs - 1

    barrier = pltpu.get_barrier_semaphore()

    @pl.when(has_below)
    def _():
        pl.semaphore_signal(barrier, inc=1, device_id={"slab": me - 1}, device_id_type=MESH)

    @pl.when(has_above)
    def _():
        pl.semaphore_signal(barrier, inc=1, device_id={"slab": me + 1}, device_id_type=MESH)

    for j in range(1, group):
        pl.semaphore_signal(
            barrier, inc=1, device_id={"shot": lax.rem(mine + j, group)}, device_id_type=MESH
        )

    inner = pl.ds(1, depth)
    pairs = [
        (pressure_hbm, fields.at[0, :, inner]),
        (density_hbm, density.at[inner]),
        (speed_hbm, pres),
        (admittance_hbm, damp),
        (mask_hbm, mask),
        (cells_hbm, cells),
        (live_hbm, live),
        (encoder_hbm, encoder),
        (target_hbm, target),
        (adjoint_hbm, adjoint),
    ]
    loads = [pltpu.make_async_copy(a, b, load_sem.at[i]) for i, (a, b) in enumerate(pairs)]
    for load in loads:
        load.start()

    def halo(k, s, source, into, first, last):
        down = pltpu.make_async_remote_copy(
            src_ref=source.at[s, pl.ds(first, 1)],
            dst_ref=into.at[s, pl.ds(depth + 1, 1)],
            send_sem=send_sem.at[k, s, 0],
            recv_sem=recv_sem.at[k, s, 0],
            device_id={"slab": me - 1},
            device_id_type=MESH,
        )
        up = pltpu.make_async_remote_copy(
            src_ref=source.at[s, pl.ds(last, 1)],
            dst_ref=into.at[s, pl.ds(0, 1)],
            send_sem=send_sem.at[k, s, 1],
            recv_sem=recv_sem.at[k, s, 1],
            device_id={"slab": me + 1},
            device_id_type=MESH,
        )
        return down, up

    def start(pair):
        down, up = pair

        @pl.when(has_below)
        def _():
            down.start()

        @pl.when(has_above)
        def _():
            up.start()

    def arrive(pair):
        down, up = pair

        @pl.when(has_above)
        def _():
            down.wait_recv()

        @pl.when(has_below)
        def _():
            up.wait_recv()

    def sent(pair):
        down, up = pair

        @pl.when(has_below)
        def _():
            down.wait_send()

        @pl.when(has_above)
        def _():
            up.wait_send()

    each = range(shots)
    rounds = [[halo(0, s, fields.at[0], fields.at[0], 1, depth) for s in each]]
    if steps > 1:
        rounds.append([halo(1, s, early, fields.at[1], 0, 1) for s in each])
    for n in range(2, steps):
        rounds.append([halo(n, s, fields.at[n], fields.at[n], 1, depth) for s in each])
    for k in range(steps - 2):
        rounds.append(
            [halo(steps + k, s, weights.at[k], weights.at[k], 1, depth) for s in each]
        )
    shared = group > 1 and width_x % (8 * group) == 0
    size_x = width_x // group if shared else width_x
    share_x = pl.ds(pl.multiple_of(mine * size_x, 8), size_x) if shared else pl.ds(0, size_x)
    coef_parts = (pl.ds(0, 1), pl.ds(1, 2))
    coefs = tuple(
        pltpu.make_async_remote_copy(
            src_ref=coef_out.at[coef_parts[i], share_x],
            dst_ref=coef_in.at[coef_parts[i], share_x],
            send_sem=coef_sem.at[0, i],
            recv_sem=coef_sem.at[1, i],
            device_id={"slab": me + 2 * i - 1},
            device_id_type=MESH,
        )
        for i in range(2)
    )
    swaps = [
        tuple(
            pltpu.make_async_remote_copy(
                src_ref=coef_in.at[coef_parts[i], share_x],
                dst_ref=coef_in.at[coef_parts[i], share_x],
                send_sem=swap_sem.at[0, i, j - 1],
                recv_sem=swap_sem.at[1, i, j - 1],
                device_id={"shot": lax.rem(mine + j, group)},
                device_id_type=MESH,
            )
            for i in range(2)
        )
        for j in range(1, group if shared else 1)
    ]
    cross = tuple(
        pltpu.make_async_remote_copy(
            src_ref=cross_out.at[i],
            dst_ref=cross_in.at[i],
            send_sem=cross_sem.at[0, i],
            recv_sem=cross_sem.at[1, i],
            device_id={"slab": me + 2 * i - 1},
            device_id_type=MESH,
        )
        for i in range(2)
    )

    zero = jnp.zeros((shots, width_x, width_y), F32)

    @pl.when(jnp.logical_not(has_below))
    def _():
        vel[0] = jnp.zeros((width_x, width_y), F32)
        cross_in[1] = jnp.zeros((width_x, width_y), F32)
        for n in range(steps):
            fields[n, :, 0] = zero
        for k in range(steps - 2):
            weights[k, :, 0] = zero

    @pl.when(jnp.logical_not(has_above))
    def _():
        cross_in[0] = jnp.zeros((width_x, width_y), F32)
        for n in range(steps):
            fields[n, :, depth + 1] = zero
        for k in range(steps - 2):
            weights[k, :, depth + 1] = zero

    if steps > 1:
        weights[steps - 2, :, 0] = zero
        weights[steps - 2, :, depth + 1] = zero

    rows = lax.broadcasted_iota(jnp.int32, (width_x, width_y), 0)
    cols = lax.broadcasted_iota(jnp.int32, (width_x, width_y), 1)

    def level(q, z):
        along_x = next_x[z] * pltpu.roll(q, width_x - 1, 0) + prev_x[z] * pltpu.roll(q, 1, 0)
        along_y = next_y[z] * pltpu.roll(q, width_y - 1, 1) + prev_y[z] * pltpu.roll(q, 1, 1)
        return along_x + along_y

    def spread(ref, n, s, z):
        q = ref[n, s, z]
        along_z = vel[z] * ref[n, s, z + 1] + vel[z - 1] * ref[n, s, z - 1]
        return level(q, z) + (along_z - centre[z] * q)

    def forward(n, which, z):
        for s in which:
            base = fields[0, s, z] if n == 0 else after[n - 1, s, z - 1]
            value = base + pres[z - 1] * spread(fields, n, s, z)
            before[n, s, z - 1] = value
            value = value * damp[z - 1]
            after[n, s, z - 1] = value
            if n + 1 < steps:
                fields[n + 1, s, z] = fields[n, s, z] + value

    def backward(n, which, z):
        k = steps - 1 - n
        part = None if k == 0 and 0 in which else grads[mine, z - 1]
        for s in which:
            value = adjoint[s, z - 1] + placed[n, s, z - 1]
            if k > 0:
                value = value + spread(weights, k - 1, s, z)
            term = before[n, s, z - 1] * value
            part = term if part is None else part + term
            if n > 0:
                scaled = value * damp[z - 1]
                adjoint[s, z - 1] = scaled
                weighted = pres[z - 1] * scaled
                if k > 0:
                    weighted = weighted + weights[k - 1, s, z]
                weights[k, s, z] = weighted
        grads[mine, z - 1] = part

    def over(low, high, step):
        size = max(g for g in (1, 2, 3) if (high - low) % g == 0)

        def run(i, carry):
            for j in range(size):
                step(low + i * size + j)
            return carry

        lax.fori_loop(0, (high - low) // size, run, 0)

    edges = (1, depth)
    middle = tuple(range(2, depth))

    for load in loads[:5]:
        load.wait()

    def coefficients(z):
        rho = density[z]
        v = 0.5 / rho
        vel[z] = v
        behind_x = jnp.where(rows == 0, 0.0, pltpu.roll(v, 1, 0))
        behind_y = jnp.where(cols == 0, 0.0, pltpu.roll(v, 1, 1))
        next_x[z] = jnp.where(rows == width_x - 1, 0.0, v)
        next_y[z] = jnp.where(cols == width_y - 1, 0.0, v)
        prev_x[z] = behind_x
        prev_y[z] = behind_y
        centre[z] = 3.0 * v + behind_x + behind_y
        c = pres[z - 1]
        pres[z - 1] = 0.5 * rho * c * c
        damp[z - 1] = 1.0 - damp[z - 1] * mask[z - 1].astype(F32)

    def add_below(z):
        centre[z] = centre[z] + vel[z - 1]

    over(1, depth + 1, coefficients)
    over(2, depth + 1, add_below)
    for i, z in enumerate(edges):
        coef_out[i] = damp[z - 1] * pres[z - 1]
    coef_out[2] = vel[depth]

    pl.semaphore_wait(
        barrier, has_below.astype(jnp.int32) + has_above.astype(jnp.int32) + (group - 1)
    )
    start(coefs)
    for s in each:
        start(rounds[0][s])
    if steps > 1:
        for s in each:
            for i, (z, beside) in enumerate(((1, 2), (depth, depth - 1))):
                q = fields[0, s, z]
                near = level(q, z) + vel[min(z, beside)] * fields[0, s, beside] - centre[z] * q
                early[s, i] = q + (q + pres[z - 1] * near) * damp[z - 1]
            start(rounds[1][s])

    for load in loads[5:9]:
        load.wait()

    caps, channels = encoder.shape
    count = slots * caps
    lanes = -(-count // 128) * 128
    spare = lanes - count
    flat = [cells[pl.ds(r, 1), :] for r in range(slots)]
    if spare:
        flat.append(jnp.full((1, spare), -1, jnp.int32))
    flat = jnp.concatenate(flat, axis=1)
    plane_at = flat // width_y
    col_at = flat - plane_at * width_y
    pick_col = jnp.where(
        lax.broadcasted_iota(jnp.int32, (width_y, lanes), 0) == col_at, 1.0, 0.0
    ).astype(jnp.bfloat16)
    read_col = jnp.concatenate([pick_col, pick_col], axis=0)
    write_col = jnp.concatenate([pick_col, pick_col], axis=1)
    plane_twice = jnp.concatenate([plane_at, plane_at], axis=1)
    band = lax.broadcasted_iota(jnp.int32, (width_x, lanes), 0)
    band_twice = lax.broadcasted_iota(jnp.int32, (width_x, 2 * lanes), 0)

    pad = -(-slots * shots // 8) * 8
    slot_of = lax.broadcasted_iota(jnp.int32, (1, lanes), 1) // caps
    row_of = lax.broadcasted_iota(jnp.int32, (pad, lanes), 0)
    owns = [row_of == slot_of * shots + s for s in range(shots)]
    row_at = lax.broadcasted_iota(jnp.int32, (pad, channels), 0)
    live_row = jnp.zeros((pad, channels), F32)
    live_lane = jnp.zeros((1, lanes), F32)
    for r in range(slots):
        alive = live[r].astype(F32)
        live_row = jnp.where(row_at // shots == r, alive, live_row)
        live_lane = jnp.where(slot_of == r, alive, live_lane)
    filters = [encoder[...]] * slots
    if spare:
        filters.append(jnp.zeros((spare, channels), F32))
    filters = jnp.concatenate(filters, axis=0)

    def exact(a, b, contract):
        return lax.dot_general(
            a,
            b,
            (contract, ((), ())),
            precision=lax.Precision.HIGHEST,
            preferred_element_type=F32,
        )

    gram = exact(filters, filters, ((1,), (1,)))
    same = lax.broadcasted_iota(jnp.int32, (lanes, lanes), 0) // caps == slot_of
    gram_high, gram_low = split(jnp.where(same, gram, 0.0))
    gram = jnp.concatenate([gram_high, gram_high, gram_low], axis=0)

    goals = []
    for n in range(steps):
        signal = jnp.zeros((pad, channels), F32)
        for r in range(slots):
            for s in range(shots):
                signal = jnp.where(row_at == r * shots + s, target[r, s, pl.ds(n, 1), :], signal)
        wide = exact(signal * live_row, filters, ((1,), (1,)))
        goals.append(
            [
                jnp.sum(jnp.where(owns[s], wide, 0.0), axis=0, keepdims=True)
                for s in range(shots)
            ]
        )

    def sample(n, planes):
        values = jnp.concatenate([after[n, s, z - 1] for s in each for z in planes], axis=0)
        got = jnp.dot(
            jnp.concatenate(split(values), axis=1), read_col, preferred_element_type=F32
        )
        found = []
        at = 0
        for s in each:
            part = jnp.zeros((width_x, lanes), F32)
            for z in planes:
                pick = band + (z - 1) * width_x == plane_at
                part = part + jnp.where(pick, got[at : at + width_x], 0.0)
                at += width_x
            found.append(jnp.sum(part, axis=0, keepdims=True))
        return found

    def encode(n, found):
        table = jnp.zeros((pad, lanes), F32)
        for s in range(shots):
            table = jnp.where(owns[s], found[s], table)
        encoded = exact(table, filters, ((1,), (0,))) * live_row
        for r in range(slots):
            for s in range(shots):
                i = r * shots + s
                record[r, s, pl.ds(n, 1), :] = encoded[i : i + 1]

    def source(n, found):
        rows_of = lax.broadcasted_iota(jnp.int32, (-(-shots // 16) * 16, lanes), 0)
        table = jnp.zeros(rows_of.shape, F32)
        for s in each:
            table = jnp.where(rows_of == s, found[s], table)
        high, low = split(table)
        wide = jnp.dot(
            jnp.concatenate([high, low, high], axis=1), gram, preferred_element_type=F32
        )
        return [wide[s : s + 1] * live_lane - goals[n][s] for s in each]

    def place(n, values, planes):
        spots = []
        for s in each:
            high, low = split(values[s])
            both = jnp.concatenate([high.astype(F32), low.astype(F32)], axis=1)
            for z in planes:
                pick = band_twice + (z - 1) * width_x == plane_twice
                spots.append(jnp.where(pick, both, 0.0).astype(jnp.bfloat16))
        put = lax.dot_general(
            jnp.concatenate(spots, axis=0),
            write_col,
            (((1,), (1,)), ((), ())),
            preferred_element_type=F32,
        )
        at = 0
        for s in each:
            for z in planes:
                placed[n, s, z - 1] = put[at : at + width_x]
                at += width_x

    last = steps - 1
    for n in range(steps):
        over(2, depth, functools.partial(forward, n, each))
        if n == last:
            found = sample(n, middle)
            olds = []
            for m in range(last):
                olds.append(sample(m, middle + edges))
                place(m, source(m, olds[m]), middle + edges)
            loads[9].wait()
        if n == 0:
            arrive(coefs)

            @pl.when(has_above)
            def _():
                for pair in swaps:
                    pair[0].start()

            @pl.when(has_below)
            def _():
                for pair in swaps:
                    pair[1].start()

            for pair in swaps:
                arrive(pair)

            @pl.when(has_below)
            def _():
                vel[0] = coef_in[2]
                add_below(1)

        for s in each:
            arrive(rounds[n][s])
        if n == 1:

            @pl.when(has_above)
            def _():
                rate = coef_in[0] * vel[depth]
                for s in each:
                    fields[1, s, depth + 1] = fields[1, s, depth + 1] + rate * (
                        fields[0, s, depth] - fields[0, s, depth + 1]
                    )

            @pl.when(has_below)
            def _():
                rate = coef_in[1] * vel[0]
                for s in each:
                    fields[1, s, 0] = fields[1, s, 0] + rate * fields[0, s, 1]

        for z in edges:
            forward(n, each, z)
        if 0 < n < last:
            for s in each:
                start(rounds[n + 1][s])

    found = [a + b for a, b in zip(found, sample(last, edges))]
    sources = source(last, found)
    place(last, sources, edges)
    for z in edges:
        backward(last, each, z)

    def send_cross():
        for i, (z, beyond) in enumerate(((1, 0), (depth, depth + 1))):
            part = None
            for s in each:
                term = weights[steps - 2, s, z] * (fields[1, s, beyond] - fields[0, s, beyond])
                part = term if part is None else part + term
            cross_out[i] = part
        start(cross)

    if last > 1:
        for s in each:
            start(rounds[steps][s])
    elif last == 1:
        send_cross()

    def share(k, low, size):
        planes = pl.ds(low, size)
        copies = []
        for j in range(1, group):
            copies.append(
                pltpu.make_async_remote_copy(
                    src_ref=grads.at[mine, planes],
                    dst_ref=grads.at[mine, planes],
                    send_sem=gsend_sem.at[k, j - 1],
                    recv_sem=grecv_sem.at[k, j - 1],
                    device_id={"shot": lax.rem(mine + j, group)},
                    device_id_type=MESH,
                )
            )
        return copies

    parts = [(1, depth - 2), (0, 1), (depth - 1, 1)]
    shares = [share(k, low, size) for k, (low, size) in enumerate(parts)]

    place(last, sources, middle)
    over(2, depth, functools.partial(backward, last, each))
    for n in reversed(range(last)):
        k = last - n
        if n == 0:
            over(1, depth + 1, functools.partial(backward, n, each))
            for copy in shares[0]:
                copy.start()
        else:
            over(2, depth, functools.partial(backward, n, each))
            for s in each:
                arrive(rounds[steps + k - 1][s])
            for z in edges:
                backward(n, each, z)
            if n > 1:
                for s in each:
                    start(rounds[steps + k][s])
            else:
                send_cross()
        encode(n, olds[n])
    encode(last, found)
    if last > 0:
        ratios = [vel[face] / damp[z - 1] for z, face in ((depth, depth), (1, 0))]
        for i, z in enumerate((depth, 1)):
            pl.when(has_below if i else has_above)(cross[i].wait_recv)
            grads[mine, z - 1] = grads[mine, z - 1] + ratios[i] * cross_in[i]
            for copy in shares[2 - i]:
                copy.start()
    else:
        for copies in shares:
            for copy in copies:
                copy.start()

    for k, (low, size) in enumerate(parts):
        for copy in shares[k]:
            copy.wait_recv()
        planes = pl.ds(low, size)
        value = grads[0, planes]
        for t in range(1, group):
            value = value + grads[t, planes]
        total[planes] = -(mask[planes].astype(F32) * value)
    for pairs in rounds:
        for pair in pairs:
            sent(pair)

    if last > 0:
        sent(cross)
    sent(coefs)

    @pl.when(has_above)
    def _():
        for pair in swaps:
            pair[0].wait_send()

    @pl.when(has_below)
    def _():
        for pair in swaps:
            pair[1].wait_send()

    for copies in shares:
        for copy in copies:
            copy.wait_send()


def deliver(record, total, record_hbm, total_hbm, sem):
    copies = [
        pltpu.make_async_copy(total, total_hbm, sem.at[0]),
        pltpu.make_async_copy(record, record_hbm, sem.at[1]),
    ]
    for copy in copies:
        copy.start()
    for copy in copies:
        copy.wait()


def solution(mesh):
    slabs, group = mesh.shape["slab"], mesh.shape["shot"]

    def body(
        pressure_init,
        adjoint_init,
        density,
        speed,
        admittance,
        bound_mask,
        rec_cells,
        rec_live,
        encoder,
        target,
    ):
        shots, depth, width_x, width_y = pressure_init.shape
        slots, caps = rec_cells.shape
        steps, channels = target.shape[2], target.shape[3]
        plane = (depth, width_x, width_y)
        padded = (shots, depth + 2, width_x, width_y)
        any_spec = pl.BlockSpec(memory_space=pl.ANY)
        vmem_spec = pl.BlockSpec(memory_space=pltpu.VMEM)

        def in_hbm(value):
            return pltpu.with_memory_space_constraint(value, pltpu.HBM)

        record, total = pl.pallas_call(
            functools.partial(kernel, slabs, group, steps, slots),
            out_shape=(
                pltpu.VMEM(target.shape, F32),
                pltpu.VMEM(plane, F32),
            ),
            in_specs=[any_spec] * 10,
            out_specs=(vmem_spec, vmem_spec),
            scratch_shapes=[
                pltpu.VMEM((steps,) + padded, F32),
                pltpu.VMEM((max(steps - 1, 1),) + padded, F32),
                pltpu.VMEM((depth + 1, width_x, width_y), F32),
                pltpu.VMEM((depth + 1, width_x, width_y), F32),
                pltpu.VMEM((depth + 1, width_x, width_y), F32),
                pltpu.VMEM((depth + 1, width_x, width_y), F32),
                pltpu.VMEM((depth + 1, width_x, width_y), F32),
                pltpu.VMEM((depth + 1, width_x, width_y), F32),
                pltpu.VMEM((depth + 1, width_x, width_y), F32),
                pltpu.VMEM(plane, F32),
                pltpu.VMEM(plane, F32),
                pltpu.VMEM(plane, jnp.int32),
                pltpu.VMEM((shots,) + plane, F32),
                pltpu.VMEM((steps, shots) + plane, F32),
                pltpu.VMEM((steps, shots) + plane, F32),
                pltpu.VMEM((steps, shots) + plane, F32),
                pltpu.VMEM((group,) + plane, F32),
                pltpu.VMEM((2, width_x, width_y), F32),
                pltpu.VMEM((2, width_x, width_y), F32),
                pltpu.VMEM((shots, 2, width_x, width_y), F32),
                pltpu.VMEM((3, width_x, width_y), F32),
                pltpu.VMEM((3, width_x, width_y), F32),
                pltpu.VMEM((slots, caps), jnp.int32),
                pltpu.SMEM((slots,), jnp.int32),
                pltpu.VMEM((caps, channels), F32),
                pltpu.VMEM(target.shape, F32),
                pltpu.SemaphoreType.DMA((10,)),
                pltpu.SemaphoreType.DMA((2 * steps, shots, 3)),
                pltpu.SemaphoreType.DMA((2 * steps, shots, 3)),
                pltpu.SemaphoreType.DMA((3, max(group - 1, 1))),
                pltpu.SemaphoreType.DMA((3, max(group - 1, 1))),
                pltpu.SemaphoreType.DMA((2, 2, max(group - 1, 1))),
                pltpu.SemaphoreType.DMA((2, 2)),
                pltpu.SemaphoreType.DMA((2, 2)),
            ],
            compiler_params=pltpu.CompilerParams(
                collective_id=0, has_side_effects=True, vmem_limit_bytes=48 * 1024 * 1024
            ),
        )(
            in_hbm(pressure_init),
            in_hbm(adjoint_init),
            in_hbm(density),
            in_hbm(speed),
            in_hbm(admittance),
            in_hbm(bound_mask),
            in_hbm(rec_cells),
            in_hbm(rec_live),
            in_hbm(encoder),
            in_hbm(target),
        )
        return pl.pallas_call(
            deliver,
            out_shape=(
                jax.ShapeDtypeStruct(target.shape, F32),
                jax.ShapeDtypeStruct(plane, F32),
            ),
            in_specs=[vmem_spec] * 2,
            out_specs=(any_spec, any_spec),
            scratch_shapes=[pltpu.SemaphoreType.DMA((2,))],
        )(
            pltpu.with_memory_space_constraint(record, pltpu.VMEM),
            pltpu.with_memory_space_constraint(total, pltpu.VMEM),
        )

    placed = (
        P("shot", "slab", None, None),
        P("shot", "slab", None, None),
        P("slab", None, None),
        P("slab", None, None),
        P("slab", None, None),
        P("slab", None, None),
        P("slab", None),
        P("slab"),
        P(),
        P("slab", "shot", None, None),
    )
    return jax.shard_map(
        body,
        mesh=mesh,
        in_specs=placed,
        out_specs=(P("slab", "shot", None, None), P("slab", None, None)),
        check_vma=False,
    )
```
